512 devices in a mesh: vocab: 64 (over x, z, core), rep: 8 (over y).
Axes of the slice: x: 4, y: 8, z: 8, core: 2. Of those that a mesh axis runs over, the one named last changes fastest.
Arguments:
- token_ids: int32 [65536], P(('vocab', 'rep')), may hold values from 0 to 8191, as said below
- cotangent: bfloat16 [65536, 4608], P(('vocab', 'rep')), may hold values from -0.059814453 to 0.059814453
- embed_table: bfloat16 [8192, 4608], P('vocab'), may hold values from -0.36 to 0.36
- norm_gain: float32 [4608], replicated, may hold values from 0.1 to 1.9
- moment_one: float32 [8192, 4608], P(('vocab', 'rep')), may hold values from -3 to 3
- moment_two: float32 [8192, 4608], P(('vocab', 'rep')), may hold values from 0.05 to 5
Outputs:
- new_table: bfloat16 [8192, 4608], P('vocab')
- new_moment_one: float32 [8192, 4608], P(('vocab', 'rep'))
- new_moment_two: float32 [8192, 4608], P(('vocab', 'rep'))
The draws below stay inside these ranges and needn't reach their ends.
Inputs may be any that keep to these rules, and one draw needn't show every extreme that they name: `token_ids`: the ids of one device fall at most 4 times into each vocabulary shard (ids s * 128 to (s + 1) * 128 - 1); in every draw some shard receives exactly 4 ids from every device.
All inputs are finite; a program needn't handle non-finite values.
Results may differ from the reference program's by a relative error of at most 0.003.
Values may be sent and summed in bfloat16 or wider, within the bound.
No kernel may reach another device: no remote copies, remote signals or barrier semaphores. Data moves between devices by JAX's collectives and lax.ppermute only.
A program may use at most 64 MiB of HBM per device.

```python
import math
import jax
import jax.numpy as jnp
from jax import lax

D = 4608
TOK_DEV = 128
CAP = 4
ROWS = 128
VOCAB = 8192
TOKENS = 65536
N_VOCAB = 64
N_REP = 8


def draw_token_ids(key, part):
    key = jax.random.fold_in(key, 11)
    key_hot, key_fill, key_row, key_perm = jax.random.split(key, 4)
    block_count = N_VOCAB * N_REP
    hot_owner = jax.random.randint(key_hot, (), 0, N_VOCAB, dtype=jnp.int32)
    pool_size = (N_VOCAB - 1) * CAP

    def one_block(block_key):
        key_order, key_shuffle = jax.random.split(block_key)
        order = jax.random.permutation(key_order, pool_size)[:TOK_DEV - CAP].astype(jnp.int32)
        others = order // CAP
        others = others + (others >= hot_owner).astype(jnp.int32)
        owners = jnp.concatenate([jnp.zeros((CAP,), jnp.int32) + hot_owner, others])
        return jax.random.permutation(key_shuffle, owners).astype(jnp.int32)
    owners = jax.vmap(one_block)(jax.random.split(key_fill, block_count)).reshape(-1)
    draws = jax.random.randint(key_row, (3, TOKENS), 0, ROWS, dtype=jnp.int32)
    lowest = jnp.min(draws, axis=0)
    row_order = jax.random.permutation(key_perm, ROWS).astype(jnp.int32)
    return (owners * ROWS + row_order[lowest]).astype(jnp.int32)


def draw_embed_table(key, part):
    key = jax.random.fold_in(key, 23)
    key_rows, key_cols, key_base = jax.random.split(key, 3)
    col_low = math.log(0.3)
    col_high = math.log(3.0)
    base = jnp.clip(jax.random.normal(key_base, (VOCAB, D), jnp.float32), -4.0, 4.0)
    row_scale = jnp.exp(jax.random.uniform(key_rows, (VOCAB, 1), jnp.float32, math.log(0.3), math.log(3.0)))
    col_scale = jnp.exp(jax.random.uniform(key_cols, (1, D), jnp.float32, col_low, col_high))
    return (0.01 * base * row_scale * col_scale).astype(jnp.bfloat16)


def levels(own_key, extent, cuts, smallest, largest):
    factor_of, own = 1.0, jax.random.fold_in(own_key, 6)
    for dim, blocks in cuts:
        steps = jnp.exp(jax.random.uniform(jax.random.fold_in(own, dim), (blocks,), jnp.float32, smallest / len(cuts), largest / len(cuts)))
        factor_of = factor_of * jnp.repeat(steps, extent[dim] // blocks).reshape([-1 if axis == dim else 1 for axis in range(len(extent))])
    return factor_of


def bell_draw(stream_key, shape, spread, most, cuts=(), kind=jnp.bfloat16):
    array = spread * jax.random.normal(stream_key, shape, jnp.float32)
    if cuts:
        array = array * levels(stream_key, shape, cuts, -0.22, 0.18)
    return jnp.clip(array, -most, most).astype(kind)


def setup_inputs(seed: int = 0) -> dict:
    splits = jax.random.split(jax.random.key(seed), 7)
    token_ids = draw_token_ids(jax.random.fold_in(splits[6], 71), 0)
    cotangent = bell_draw(splits[1], (TOKENS, D), 0.01, 0.059814453, ((0, 512),))
    embed_table = draw_embed_table(jax.random.fold_in(splits[6], 71), 0)
    norm_gain = jnp.clip(1.0 + 0.18 * jax.random.normal(splits[3], (D,), jnp.float32), 0.1, 1.9)
    moment_one = bell_draw(splits[4], (VOCAB, D), 0.5, 3.0, ((0, 512),), jnp.float32)
    moment_two = jnp.clip(jnp.exp(math.log(5.0) - 4.6051702 * jax.random.uniform(splits[5], (VOCAB, D), jnp.float32) ** levels(splits[5], (VOCAB, D), ((0, 512),), -0.2, 0.2)), 0.05, 5.0)
    return {"token_ids": token_ids, "cotangent": cotangent, "embed_table": embed_table, "norm_gain": norm_gain, "moment_one": moment_one, "moment_two": moment_two}


beta_one = 0.9
beta_two = 0.95
learn_rate = 0.01
decay_rate = 0.01
adam_eps = 1e-08
norm_eps = 1e-06
correct_one = 0.9999734386011124
correct_two = 0.9940794707920236

def token_grads(fetched_rows, cotangent, norm_gain):
    width = fetched_rows.shape[-1]
    root = math.sqrt(width)
    scaled = fetched_rows.astype(jnp.float32) * root
    weighted = cotangent.astype(jnp.float32) * norm_gain.astype(jnp.float32)
    mean_square = lax.optimization_barrier(jnp.mean(scaled * scaled, axis=-1, keepdims=True))
    inverse = lax.rsqrt(mean_square + norm_eps)
    inner_mean = lax.optimization_barrier(jnp.mean(scaled * weighted, axis=-1, keepdims=True))
    return (root * inverse * (weighted - scaled * inverse * inverse * inner_mean)).astype(jnp.bfloat16)

def reference(token_ids, cotangent, embed_table, norm_gain, moment_one, moment_two):
    group_size = TOKENS // N_REP
    id_blocks = token_ids.reshape(N_REP, group_size)
    cot_blocks = cotangent.reshape(N_REP, group_size, D)

    def add_block(totals, pieces):
        block_ids, block_cot = pieces
        fetched_rows = jnp.take(embed_table, block_ids, axis=0)
        token_grad = token_grads(fetched_rows, block_cot, norm_gain).astype(jnp.float32)
        return (totals + jax.ops.segment_sum(token_grad, block_ids, num_segments=VOCAB), None)
    row_grad, _ = lax.scan(add_block, jnp.zeros((VOCAB, D), jnp.float32), (id_blocks, cot_blocks))
    new_moment_one = beta_one * moment_one + (1.0 - beta_one) * row_grad
    new_moment_two = beta_two * moment_two + (1.0 - beta_two) * row_grad * row_grad
    params = embed_table.astype(jnp.float32)
    update = new_moment_one / correct_one / (jnp.sqrt(new_moment_two / correct_two) + adam_eps) + decay_rate * params
    new_table = (params - learn_rate * update).astype(jnp.bfloat16)
    return (new_table, new_moment_one, new_moment_two)
```

```python
import math

import jax
import jax.numpy as jnp
from jax import lax
from jax.experimental import pallas as pl
from jax.experimental.pallas import tpu as pltpu
from jax.sharding import PartitionSpec as P

beta_one = 0.9
beta_two = 0.95
learn_rate = 0.01
decay_rate = 0.01
adam_eps = 1e-08
norm_eps = 1e-06
correct_one = 0.9999734386011124
correct_two = 0.9940794707920236

SLOTS = 4
LANES = 128
GATHERED = 3968


def pack_body(ids_ref, cot_ref, out_ref):
    tok_count, width = cot_ref.shape
    half = width // 2
    block_rows = out_ref.shape[0]
    ids_along = jnp.broadcast_to(ids_ref[...], (tok_count, tok_count))
    ids_down = ids_along.T
    down = lax.broadcasted_iota(jnp.int32, (tok_count, tok_count), 0)
    along = lax.broadcasted_iota(jnp.int32, (tok_count, tok_count), 1)
    earlier = ((ids_along >> 7) == (ids_down >> 7)) & (down < along)
    position = jnp.sum(earlier.astype(jnp.int32), axis=0, keepdims=True)
    slot = (ids_ref[...] >> 7) * (2 * SLOTS) + position
    slots = jnp.concatenate([slot, slot + SLOTS], axis=1)
    rows = lax.broadcasted_iota(jnp.int32, (block_rows, 2 * tok_count), 0)
    rows = rows + pl.program_id(0) * block_rows
    picks = (rows == slots).astype(jnp.bfloat16)
    halves = jnp.concatenate([cot_ref[:, :half], cot_ref[:, half:]], axis=0)
    out_ref[:, :half] = jnp.dot(picks, halves, preferred_element_type=jnp.float32).astype(
        jnp.bfloat16
    )
    marks = ((ids_down & (LANES - 1)) == along).astype(jnp.bfloat16)
    marks = jnp.concatenate([marks, marks], axis=0)
    out_ref[:, half:] = jnp.dot(picks, marks, preferred_element_type=jnp.float32).astype(
        jnp.bfloat16
    )


def pack(token_ids, cotangent, peer_count):
    tok_count, width = cotangent.shape
    lanes = width // 2 + LANES
    rows = peer_count * 2 * SLOTS
    steps = 4
    return pl.pallas_call(
        pack_body,
        grid=(steps,),
        in_specs=[
            pl.BlockSpec((1, tok_count), lambda i: (0, 0)),
            pl.BlockSpec((tok_count, width), lambda i: (0, 0)),
        ],
        out_specs=pl.BlockSpec((rows // steps, lanes), lambda i: (i, 0)),
        out_shape=jax.ShapeDtypeStruct((rows, lanes), jnp.bfloat16),
        compiler_params=pltpu.CompilerParams(vmem_limit_bytes=40 * 1024 * 1024),
        cost_estimate=pl.CostEstimate(
            flops=2 * rows * 2 * tok_count * lanes,
            bytes_accessed=2 * (tok_count * width + rows * lanes),
            transcendentals=0,
        ),
        name="pack",
    )(token_ids.reshape(1, tok_count), cotangent)


def collect_body(marks_ref, part_ref, out_ref):
    count, part = part_ref.shape
    half = out_ref.shape[1] // 2
    which = lax.broadcasted_iota(jnp.int32, (count, LANES), 0) & SLOTS
    marks = marks_ref[...].astype(jnp.float32)
    first = jnp.where(which == 0, marks, 0.0)
    second = jnp.where(which == 0, 0.0, marks)
    picks = jnp.concatenate([first.T, second.T], axis=0).astype(jnp.bfloat16)
    sums = jnp.dot(picks, part_ref[...], preferred_element_type=jnp.float32)
    at = pl.multiple_of(pl.program_id(0) * part, LANES)
    out_ref[:, pl.ds(at, part)] = sums[:LANES]
    out_ref[:, pl.ds(half + at, part)] = sums[LANES:]


def collect(arrived):
    count, lanes = arrived.shape
    half = lanes - LANES
    steps = 3
    part = half // steps
    return pl.pallas_call(
        collect_body,
        grid=(steps,),
        in_specs=[
            pl.BlockSpec((count, LANES), lambda i: (0, half // LANES)),
            pl.BlockSpec((count, part), lambda i: (0, i)),
        ],
        out_specs=pl.BlockSpec((LANES, 2 * half), lambda i: (0, 0)),
        out_shape=jax.ShapeDtypeStruct((LANES, 2 * half), jnp.float32),
        compiler_params=pltpu.CompilerParams(vmem_limit_bytes=40 * 1024 * 1024),
        cost_estimate=pl.CostEstimate(
            flops=2 * count * 2 * LANES * half,
            bytes_accessed=2 * count * lanes + 8 * LANES * half,
            transcendentals=0,
        ),
        name="collect",
    )(arrived, arrived)


def adam_body(rep_ref, sum_ref, table_ref, gain_ref, one_ref, two_ref, up_ref, rest_ref, one_out, two_out):
    width = sum_ref.shape[1]
    root = math.sqrt(width)
    params = table_ref[...].astype(jnp.float32)
    scaled = params * root
    weighted = sum_ref[...] * gain_ref[...]
    mean_square = jnp.mean(scaled * scaled, axis=-1, keepdims=True)
    inverse = lax.rsqrt(mean_square + norm_eps)
    inner_mean = jnp.mean(scaled * weighted, axis=-1, keepdims=True)
    grad = root * inverse * (weighted - scaled * (inverse * inverse * inner_mean))
    new_one = beta_one * one_ref[...] + (1.0 - beta_one) * grad
    new_two = beta_two * two_ref[...] + (1.0 - beta_two) * grad * grad
    one_out[...] = new_one
    two_out[...] = new_two
    update = (
        new_one / correct_one / (jnp.sqrt(new_two / correct_two) + adam_eps) + decay_rate * params
    )
    updated = (params - learn_rate * update).astype(jnp.bfloat16)
    up_ref[...] = updated[:, :GATHERED]
    rest = updated[:, GATHERED:]
    rows = rest.shape[0]
    for peer in range(rest_ref.shape[0] // rows):
        rest_ref[peer * rows : (peer + 1) * rows, :] = rest


def adam(rep_index, slice_sum, embed_table, norm_gain, moment_one, moment_two):
    rows, width = slice_sum.shape
    peers = embed_table.shape[0] // rows
    whole = pl.BlockSpec((rows, width), lambda i, rep: (0, 0))
    return pl.pallas_call(
        adam_body,
        grid_spec=pltpu.PrefetchScalarGridSpec(
            num_scalar_prefetch=1,
            grid=(1,),
            in_specs=[
                whole,
                pl.BlockSpec((rows, width), lambda i, rep: (rep[0], 0)),
                pl.BlockSpec((1, width), lambda i, rep: (0, 0)),
                whole,
                whole,
            ],
            out_specs=[
                pl.BlockSpec((rows, GATHERED), lambda i, rep: (0, 0)),
                pl.BlockSpec((peers * rows, width - GATHERED), lambda i, rep: (0, 0)),
                whole,
                whole,
            ],
        ),
        out_shape=[
            jax.ShapeDtypeStruct((rows, GATHERED), jnp.bfloat16),
            jax.ShapeDtypeStruct((peers * rows, width - GATHERED), jnp.bfloat16),
            jax.ShapeDtypeStruct((rows, width), jnp.float32),
            jax.ShapeDtypeStruct((rows, width), jnp.float32),
        ],
        compiler_params=pltpu.CompilerParams(vmem_limit_bytes=40 * 1024 * 1024),
        cost_estimate=pl.CostEstimate(
            flops=40 * rows * width, bytes_accessed=24 * rows * width, transcendentals=rows * width
        ),
        name="adam",
    )(rep_index, slice_sum, embed_table, norm_gain.reshape(1, width), moment_one, moment_two)


def on_device(token_ids, cotangent, embed_table, norm_gain, moment_one, moment_two):
    peer_count = lax.axis_size("vocab")
    outgoing = pack(token_ids, cotangent, peer_count)
    arrived = lax.all_to_all(outgoing, "vocab", split_axis=0, concat_axis=0, tiled=True)
    row_sum = collect(arrived)
    slice_sum = lax.psum_scatter(row_sum, "rep", scatter_dimension=0, tiled=True)
    rep_index = lax.axis_index("rep").astype(jnp.int32).reshape(1)
    updated, rest, new_moment_one, new_moment_two = adam(
        rep_index, slice_sum, embed_table, norm_gain, moment_one, moment_two
    )
    left = lax.all_gather(updated, "rep", axis=0, tiled=True)
    right = lax.all_to_all(rest, "rep", split_axis=0, concat_axis=0, tiled=True)
    new_table = jnp.concatenate([left, right], axis=1)
    return (new_table, new_moment_one, new_moment_two)


def solution(mesh):
    placed = (
        P(("vocab", "rep")),
        P(("vocab", "rep"), None),
        P("vocab", None),
        P(),
        P(("vocab", "rep"), None),
        P(("vocab", "rep"), None),
    )
    return jax.shard_map(
        on_device,
        mesh=mesh,
        in_specs=placed,
        out_specs=(P("vocab", None), P(("vocab", "rep"), None), P(("vocab", "rep"), None)),
        check_vma=False,
    )
```

```python
import math

import jax
import jax.numpy as jnp
from jax import lax
from jax.experimental import pallas as pl
from jax.experimental.pallas import tpu as pltpu
from jax.sharding import PartitionSpec as P

beta_one = 0.9
beta_two = 0.95
learn_rate = 0.01
decay_rate = 0.01
adam_eps = 1e-08
norm_eps = 1e-06
correct_one = 0.9999734386011124
correct_two = 0.9940794707920236

SLOTS = 4
LANES = 128
GATHERED = 3968


def pack_body(ids_ref, cot_ref, out_ref):
    tok_count, width = cot_ref.shape
    half = width // 2
    block_rows = out_ref.shape[0]
    ids_along = jnp.broadcast_to(ids_ref[...], (tok_count, tok_count))
    ids_down = ids_along.T
    down = lax.broadcasted_iota(jnp.int32, (tok_count, tok_count), 0)
    along = lax.broadcasted_iota(jnp.int32, (tok_count, tok_count), 1)
    earlier = ((ids_along >> 7) == (ids_down >> 7)) & (down < along)
    position = jnp.sum(earlier.astype(jnp.int32), axis=0, keepdims=True)
    slot = (ids_ref[...] >> 7) * (2 * SLOTS) + position
    slots = jnp.concatenate([slot, slot + SLOTS], axis=1)
    rows = lax.broadcasted_iota(jnp.int32, (block_rows, 2 * tok_count), 0)
    rows = rows + pl.program_id(0) * block_rows
    picks = (rows == slots).astype(jnp.bfloat16)
    halves = jnp.concatenate([cot_ref[:, :half], cot_ref[:, half:]], axis=0)
    out_ref[:, :half] = jnp.dot(picks, halves, preferred_element_type=jnp.float32).astype(
        jnp.bfloat16
    )
    marks = ((ids_down & (LANES - 1)) == along).astype(jnp.bfloat16)
    marks = jnp.concatenate([marks, marks], axis=0)
    out_ref[:, half:] = jnp.dot(picks, marks, preferred_element_type=jnp.float32).astype(
        jnp.bfloat16
    )


def pack(token_ids, cotangent, peer_count):
    tok_count, width = cotangent.shape
    lanes = width // 2 + LANES
    rows = peer_count * 2 * SLOTS
    steps = 4
    return pl.pallas_call(
        pack_body,
        grid=(steps,),
        in_specs=[
            pl.BlockSpec((1, tok_count), lambda i: (0, 0)),
            pl.BlockSpec((tok_count, width), lambda i: (0, 0)),
        ],
        out_specs=pl.BlockSpec((rows // steps, lanes), lambda i: (i, 0)),
        out_shape=jax.ShapeDtypeStruct((rows, lanes), jnp.bfloat16),
        compiler_params=pltpu.CompilerParams(vmem_limit_bytes=40 * 1024 * 1024),
        cost_estimate=pl.CostEstimate(
            flops=2 * rows * 2 * tok_count * lanes,
            bytes_accessed=2 * (tok_count * width + rows * lanes),
            transcendentals=0,
        ),
        name="pack",
    )(token_ids.reshape(1, tok_count), cotangent)


def collect_body(marks_ref, part_ref, out_ref):
    count, part = part_ref.shape
    half = out_ref.shape[1] // 2
    which = lax.broadcasted_iota(jnp.int32, (count, LANES), 0) & SLOTS
    marks = marks_ref[...].astype(jnp.float32)
    first = jnp.where(which == 0, marks, 0.0)
    second = jnp.where(which == 0, 0.0, marks)
    picks = jnp.concatenate([first.T, second.T], axis=0).astype(jnp.bfloat16)
    sums = jnp.dot(picks, part_ref[...], preferred_element_type=jnp.float32).astype(jnp.bfloat16)
    at = pl.multiple_of(pl.program_id(0) * part, LANES)
    out_ref[:, pl.ds(at, part)] = sums[:LANES]
    out_ref[:, pl.ds(half + at, part)] = sums[LANES:]


def collect(arrived):
    count, lanes = arrived.shape
    half = lanes - LANES
    steps = 3
    part = half // steps
    return pl.pallas_call(
        collect_body,
        grid=(steps,),
        in_specs=[
            pl.BlockSpec((count, LANES), lambda i: (0, half // LANES)),
            pl.BlockSpec((count, part), lambda i: (0, i)),
        ],
        out_specs=pl.BlockSpec((LANES, 2 * half), lambda i: (0, 0)),
        out_shape=jax.ShapeDtypeStruct((LANES, 2 * half), jnp.bfloat16),
        compiler_params=pltpu.CompilerParams(vmem_limit_bytes=40 * 1024 * 1024),
        cost_estimate=pl.CostEstimate(
            flops=2 * count * 2 * LANES * half,
            bytes_accessed=2 * count * lanes + 4 * LANES * half,
            transcendentals=0,
        ),
        name="collect",
    )(arrived, arrived)


def adam_body(rep_ref, sum_ref, table_ref, gain_ref, one_ref, two_ref, up_ref, rest_ref, one_out, two_out):
    width = sum_ref.shape[1]
    root = math.sqrt(width)
    params = table_ref[...].astype(jnp.float32)
    scaled = params * root
    rows = table_ref.shape[0]
    total = sum_ref[:rows, :].astype(jnp.float32)
    for peer in range(1, sum_ref.shape[0] // rows):
        total = total + sum_ref[peer * rows : (peer + 1) * rows, :].astype(jnp.float32)
    weighted = total * gain_ref[...]
    mean_square = jnp.mean(scaled * scaled, axis=-1, keepdims=True)
    inverse = lax.rsqrt(mean_square + norm_eps)
    inner_mean = jnp.mean(scaled * weighted, axis=-1, keepdims=True)
    grad = root * inverse * (weighted - scaled * (inverse * inverse * inner_mean))
    new_one = beta_one * one_ref[...] + (1.0 - beta_one) * grad
    new_two = beta_two * two_ref[...] + (1.0 - beta_two) * grad * grad
    one_out[...] = new_one
    two_out[...] = new_two
    update = (
        new_one / correct_one / (jnp.sqrt(new_two / correct_two) + adam_eps) + decay_rate * params
    )
    updated = (params - learn_rate * update).astype(jnp.bfloat16)
    up_ref[...] = updated[:, :GATHERED]
    rest = updated[:, GATHERED:]
    for peer in range(rest_ref.shape[0] // rows):
        rest_ref[peer * rows : (peer + 1) * rows, :] = rest


def adam(rep_index, partial_sums, embed_table, norm_gain, moment_one, moment_two):
    rows, width = moment_one.shape
    peers = embed_table.shape[0] // rows
    whole = pl.BlockSpec((rows, width), lambda i, rep: (0, 0))
    return pl.pallas_call(
        adam_body,
        grid_spec=pltpu.PrefetchScalarGridSpec(
            num_scalar_prefetch=1,
            grid=(1,),
            in_specs=[
                pl.BlockSpec((peers * rows, width), lambda i, rep: (0, 0)),
                pl.BlockSpec((rows, width), lambda i, rep: (rep[0], 0)),
                pl.BlockSpec((1, width), lambda i, rep: (0, 0)),
                whole,
                whole,
            ],
            out_specs=[
                pl.BlockSpec((rows, GATHERED), lambda i, rep: (0, 0)),
                pl.BlockSpec((peers * rows, width - GATHERED), lambda i, rep: (0, 0)),
                whole,
                whole,
            ],
        ),
        out_shape=[
            jax.ShapeDtypeStruct((rows, GATHERED), jnp.bfloat16),
            jax.ShapeDtypeStruct((peers * rows, width - GATHERED), jnp.bfloat16),
            jax.ShapeDtypeStruct((rows, width), jnp.float32),
            jax.ShapeDtypeStruct((rows, width), jnp.float32),
        ],
        compiler_params=pltpu.CompilerParams(vmem_limit_bytes=40 * 1024 * 1024),
        cost_estimate=pl.CostEstimate(
            flops=40 * rows * width, bytes_accessed=24 * rows * width, transcendentals=rows * width
        ),
        name="adam",
    )(rep_index, partial_sums, embed_table, norm_gain.reshape(1, width), moment_one, moment_two)


def on_device(token_ids, cotangent, embed_table, norm_gain, moment_one, moment_two):
    peer_count = lax.axis_size("vocab")
    outgoing = pack(token_ids, cotangent, peer_count)
    arrived = lax.all_to_all(outgoing, "vocab", split_axis=0, concat_axis=0, tiled=True)
    row_sum = collect(arrived)
    partial_sums = lax.all_to_all(row_sum, "rep", split_axis=0, concat_axis=0, tiled=True)
    rep_index = lax.axis_index("rep").astype(jnp.int32).reshape(1)
    updated, rest, new_moment_one, new_moment_two = adam(
        rep_index, partial_sums, embed_table, norm_gain, moment_one, moment_two
    )
    left = lax.all_gather(updated, "rep", axis=0, tiled=True)
    right = lax.all_to_all(rest, "rep", split_axis=0, concat_axis=0, tiled=True)
    new_table = jnp.concatenate([left, right], axis=1)
    return (new_table, new_moment_one, new_moment_two)


def solution(mesh):
    placed = (
        P(("vocab", "rep")),
        P(("vocab", "rep"), None),
        P("vocab", None),
        P(),
        P(("vocab", "rep"), None),
        P(("vocab", "rep"), None),
    )
    return jax.shard_map(
        on_device,
        mesh=mesh,
        in_specs=placed,
        out_specs=(P("vocab", None), P(("vocab", "rep"), None), P(("vocab", "rep"), None)),
        check_vma=False,
    )
```

```python
import math

import jax
import jax.numpy as jnp
from jax import lax
from jax.experimental import pallas as pl
from jax.experimental.pallas import tpu as pltpu
from jax.sharding import Mesh
from jax.sharding import PartitionSpec as P

beta_one = 0.9
beta_two = 0.95
learn_rate = 0.01
decay_rate = 0.01
adam_eps = 1e-08
norm_eps = 1e-06
correct_one = 0.9999734386011124
correct_two = 0.9940794707920236

SLOTS = 4
LANES = 128
GATHERED = 3968


def pack_body(ids_ref, cot_ref, out_ref):
    tok_count, width = cot_ref.shape
    quarter = width // 4
    block_rows = out_ref.shape[0]
    ids_along = jnp.broadcast_to(ids_ref[...], (tok_count, tok_count))
    ids_down = ids_along.T
    down = lax.broadcasted_iota(jnp.int32, (tok_count, tok_count), 0)
    along = lax.broadcasted_iota(jnp.int32, (tok_count, tok_count), 1)
    earlier = ((ids_along >> 7) == (ids_down >> 7)) & (down < along)
    position = jnp.sum(earlier.astype(jnp.int32), axis=0, keepdims=True)
    slot = (ids_ref[...] >> 7) * (4 * SLOTS) + position
    slots = jnp.concatenate([slot + part * SLOTS for part in range(4)], axis=1)
    rows = lax.broadcasted_iota(jnp.int32, (block_rows, 4 * tok_count), 0)
    rows = rows + pl.program_id(0) * block_rows
    picks = (rows == slots).astype(jnp.bfloat16)
    quarters = [cot_ref[:, part * quarter : (part + 1) * quarter] for part in range(4)]
    out_ref[:, :quarter] = jnp.dot(
        picks, jnp.concatenate(quarters, axis=0), preferred_element_type=jnp.float32
    ).astype(jnp.bfloat16)
    marks = ((ids_down & (LANES - 1)) == along).astype(jnp.bfloat16)
    marks = jnp.concatenate([marks] * 4, axis=0)
    out_ref[:, quarter:] = jnp.dot(picks, marks, preferred_element_type=jnp.float32).astype(
        jnp.bfloat16
    )


def pack(token_ids, cotangent, peer_count):
    tok_count, width = cotangent.shape
    lanes = width // 4 + LANES
    rows = peer_count * 4 * SLOTS
    steps = 4
    return pl.pallas_call(
        pack_body,
        grid=(steps,),
        in_specs=[
            pl.BlockSpec((1, tok_count), lambda i: (0, 0)),
            pl.BlockSpec((tok_count, width), lambda i: (0, 0)),
        ],
        out_specs=pl.BlockSpec((rows // steps, lanes), lambda i: (i, 0)),
        out_shape=jax.ShapeDtypeStruct((rows, lanes), jnp.bfloat16),
        compiler_params=pltpu.CompilerParams(vmem_limit_bytes=40 * 1024 * 1024),
        cost_estimate=pl.CostEstimate(
            flops=2 * rows * 4 * tok_count * lanes,
            bytes_accessed=2 * (tok_count * width + rows * lanes),
            transcendentals=0,
        ),
        name="pack",
    )(token_ids.reshape(1, tok_count), cotangent)


def collect_body(marks_ref, part_ref, out_ref):
    count, part = part_ref.shape
    half = out_ref.shape[1] // 2
    which = lax.broadcasted_iota(jnp.int32, (count, LANES), 0) & SLOTS
    marks = marks_ref[...].astype(jnp.float32)
    first = jnp.where(which == 0, marks, 0.0)
    second = jnp.where(which == 0, 0.0, marks)
    picks = jnp.concatenate([first.T, second.T], axis=0).astype(jnp.bfloat16)
    sums = jnp.dot(picks, part_ref[...], preferred_element_type=jnp.float32).astype(jnp.bfloat16)
    at = pl.multiple_of(pl.program_id(0) * part, LANES)
    out_ref[:, pl.ds(at, part)] = sums[:LANES]
    out_ref[:, pl.ds(half + at, part)] = sums[LANES:]


def collect(arrived):
    count, lanes = arrived.shape
    half = lanes - LANES
    steps = 3
    part = half // steps
    return pl.pallas_call(
        collect_body,
        grid=(steps,),
        in_specs=[
            pl.BlockSpec((count, LANES), lambda i: (0, half // LANES)),
            pl.BlockSpec((count, part), lambda i: (0, i)),
        ],
        out_specs=pl.BlockSpec((LANES, 2 * half), lambda i: (0, 0)),
        out_shape=jax.ShapeDtypeStruct((LANES, 2 * half), jnp.bfloat16),
        compiler_params=pltpu.CompilerParams(vmem_limit_bytes=40 * 1024 * 1024),
        cost_estimate=pl.CostEstimate(
            flops=2 * count * 2 * LANES * half,
            bytes_accessed=2 * count * lanes + 4 * LANES * half,
            transcendentals=0,
        ),
        name="collect",
    )(arrived, arrived)


def adam_body(rep_ref, sum_ref, table_ref, gain_ref, one_ref, two_ref, up_ref, rest_ref, one_out, two_out):
    width = table_ref.shape[1]
    root = math.sqrt(width)
    params = table_ref[...].astype(jnp.float32)
    scaled = params * root
    rows = table_ref.shape[0]
    totals = []
    for member in range(2):
        total = sum_ref[member * rows : (member + 1) * rows, :].astype(jnp.float32)
        for peer in range(member + 2, sum_ref.shape[0] // rows, 2):
            total = total + sum_ref[peer * rows : (peer + 1) * rows, :].astype(jnp.float32)
        totals.append(total)
    weighted = jnp.concatenate(totals, axis=1) * gain_ref[...]
    mean_square = jnp.mean(scaled * scaled, axis=-1, keepdims=True)
    inverse = lax.rsqrt(mean_square + norm_eps)
    inner_mean = jnp.mean(scaled * weighted, axis=-1, keepdims=True)
    grad = root * inverse * (weighted - scaled * (inverse * inverse * inner_mean))
    new_one = beta_one * one_ref[...] + (1.0 - beta_one) * grad
    new_two = beta_two * two_ref[...] + (1.0 - beta_two) * grad * grad
    one_out[...] = new_one
    two_out[...] = new_two
    update = (
        new_one / correct_one / (jnp.sqrt(new_two / correct_two) + adam_eps) + decay_rate * params
    )
    updated = (params - learn_rate * update).astype(jnp.bfloat16)
    up_ref[...] = updated[:, :GATHERED]
    rest = updated[:, GATHERED:]
    for peer in range(rest_ref.shape[0] // rows):
        rest_ref[peer * rows : (peer + 1) * rows, :] = rest


def adam(rep_index, partial_sums, embed_table, norm_gain, moment_one, moment_two):
    rows, width = moment_one.shape
    peers = embed_table.shape[0] // rows
    whole = pl.BlockSpec((rows, width), lambda i, rep: (0, 0))
    return pl.pallas_call(
        adam_body,
        grid_spec=pltpu.PrefetchScalarGridSpec(
            num_scalar_prefetch=1,
            grid=(1,),
            in_specs=[
                pl.BlockSpec((peers * rows, width // 2), lambda i, rep: (0, 0)),
                pl.BlockSpec((rows, width), lambda i, rep: (rep[0], 0)),
                pl.BlockSpec((1, width), lambda i, rep: (0, 0)),
                whole,
                whole,
            ],
            out_specs=[
                pl.BlockSpec((rows, GATHERED), lambda i, rep: (0, 0)),
                pl.BlockSpec((peers * rows, width - GATHERED), lambda i, rep: (0, 0)),
                whole,
                whole,
            ],
        ),
        out_shape=[
            jax.ShapeDtypeStruct((rows, GATHERED), jnp.bfloat16),
            jax.ShapeDtypeStruct((peers * rows, width - GATHERED), jnp.bfloat16),
            jax.ShapeDtypeStruct((rows, width), jnp.float32),
            jax.ShapeDtypeStruct((rows, width), jnp.float32),
        ],
        compiler_params=pltpu.CompilerParams(vmem_limit_bytes=40 * 1024 * 1024),
        cost_estimate=pl.CostEstimate(
            flops=40 * rows * width, bytes_accessed=24 * rows * width, transcendentals=rows * width
        ),
        name="adam",
    )(rep_index, partial_sums, embed_table, norm_gain.reshape(1, width), moment_one, moment_two)


REP = ("four", "pair")
ALL = ("vocab", "four", "pair")


def on_device(token_ids, cotangent, embed_table, norm_gain, moment_one, moment_two):
    peer_count = lax.axis_size("vocab")
    outgoing = pack(token_ids, cotangent, peer_count)
    arrived = lax.all_to_all(outgoing, ("vocab", "pair"), split_axis=0, concat_axis=0, tiled=True)
    row_sum = collect(arrived)
    partial_sums = lax.all_to_all(row_sum, REP, split_axis=0, concat_axis=0, tiled=True)
    rep_index = lax.axis_index(REP).astype(jnp.int32).reshape(1)
    updated, rest, new_moment_one, new_moment_two = adam(
        rep_index, partial_sums, embed_table, norm_gain, moment_one, moment_two
    )
    left = lax.all_gather(updated, REP, axis=0, tiled=True)
    right = lax.all_to_all(rest, REP, split_axis=0, concat_axis=0, tiled=True)
    new_table = jnp.concatenate([left, right], axis=1)
    return (new_table, new_moment_one, new_moment_two)


def solution(mesh):
    vocab, rep = mesh.devices.shape
    paired = Mesh(mesh.devices.reshape(vocab, rep // 2, 2), ALL)
    placed = (
        P(ALL),
        P(ALL, None),
        P("vocab", None),
        P(),
        P(ALL, None),
        P(ALL, None),
    )
    return jax.shard_map(
        on_device,
        mesh=paired,
        in_specs=placed,
        out_specs=(P("vocab", None), P(ALL, None), P(ALL, None)),
        check_vma=False,
    )
```

```python
import math

import jax
import jax.numpy as jnp
from jax import lax
from jax.experimental import pallas as pl
from jax.experimental.pallas import tpu as pltpu
from jax.sharding import Mesh
from jax.sharding import PartitionSpec as P

beta_one = 0.9
beta_two = 0.95
learn_rate = 0.01
decay_rate = 0.01
adam_eps = 1e-08
norm_eps = 1e-06
correct_one = 0.9999734386011124
correct_two = 0.9940794707920236

SLOTS = 4
LANES = 128
GATHERED = 3968
MEMBERS = 4
HIGH = 8
LOW = 16
CODE = 64


def pack_body(ids_ref, cot_hbm, out_ref, cot_ref, piece_ref, slot_ref, sem):
    tok_count, width = cot_ref.shape
    piece = width // (2 * MEMBERS)
    lanes = out_ref.shape[-1]

    @pl.when(pl.program_id(0) == 0)
    def _():
        copy = pltpu.make_async_copy(cot_hbm, cot_ref, sem)
        copy.start()
        ids_along = jnp.broadcast_to(ids_ref[...], (tok_count, tok_count))
        ids_down = ids_along.T
        down = lax.broadcasted_iota(jnp.int32, (tok_count, tok_count), 0)
        along = lax.broadcasted_iota(jnp.int32, (tok_count, tok_count), 1)
        earlier = ((ids_along >> 7) == (ids_down >> 7)) & (down < along)
        position = jnp.sum(earlier.astype(jnp.int32), axis=0, keepdims=True)
        slot_ref[...] = (ids_ref[...] >> 7) * (2 * SLOTS) + position
        high = (ids_down >> 4) & (HIGH - 1)
        low = (ids_down & (LOW - 1)) + HIGH
        marks = ((along == high) | (along == low)).astype(jnp.bfloat16)[:, : lanes - piece]
        copy.wait()
        for at in range(2 * MEMBERS):
            member, half = at // 2, at % 2
            rows = slice(half * tok_count, (half + 1) * tok_count)
            piece_ref[member, rows, :piece] = cot_ref[:, at * piece : (at + 1) * piece]
            piece_ref[member, rows, piece:] = marks

    owners = out_ref.shape[0]
    block_rows = owners * 2 * SLOTS
    slots = jnp.concatenate([slot_ref[...], slot_ref[...] + SLOTS], axis=1)
    rows = lax.broadcasted_iota(jnp.int32, (block_rows, 2 * tok_count), 0)
    rows = rows + pl.program_id(0) * block_rows
    picks = (rows == slots).astype(jnp.bfloat16)
    for member in range(MEMBERS):
        moved = jnp.dot(picks, piece_ref[member], preferred_element_type=jnp.float32)
        out_ref[:, member] = moved.reshape(owners, 2 * SLOTS, lanes).astype(jnp.bfloat16)


def pack(token_ids, cotangent, peer_count):
    tok_count, width = cotangent.shape
    lanes = width // (2 * MEMBERS) + CODE
    steps = 4
    return pl.pallas_call(
        pack_body,
        grid=(steps,),
        in_specs=[
            pl.BlockSpec((1, tok_count), lambda i: (0, 0)),
            pl.BlockSpec(memory_space=pl.ANY),
        ],
        out_specs=pl.BlockSpec(
            (peer_count // steps, MEMBERS, 2 * SLOTS, lanes), lambda i: (i, 0, 0, 0)
        ),
        out_shape=jax.ShapeDtypeStruct((peer_count, MEMBERS, 2 * SLOTS, lanes), jnp.bfloat16),
        scratch_shapes=[
            pltpu.VMEM((tok_count, width), jnp.bfloat16),
            pltpu.VMEM((MEMBERS, 2 * tok_count, lanes), jnp.bfloat16),
            pltpu.VMEM((1, tok_count), jnp.int32),
            pltpu.SemaphoreType.DMA,
        ],
        compiler_params=pltpu.CompilerParams(vmem_limit_bytes=40 * 1024 * 1024),
        cost_estimate=pl.CostEstimate(
            flops=2 * peer_count * 2 * SLOTS * 2 * tok_count * MEMBERS * lanes,
            bytes_accessed=2 * (tok_count * width + peer_count * MEMBERS * 2 * SLOTS * lanes),
            transcendentals=0,
        ),
        name="pack",
    )(token_ids.reshape(1, tok_count), cotangent)


def collect_body(part_ref, out_ref, sum_ref):
    count, lanes = part_ref.shape
    piece = out_ref.shape[1] // 2
    step = pl.program_id(0)
    shard_row = lax.broadcasted_iota(jnp.int32, (LANES, CODE), 0)
    lane = lax.broadcasted_iota(jnp.int32, (LANES, CODE), 1)
    high = (lane == (shard_row >> 4)).astype(jnp.bfloat16)
    low = (lane == (shard_row & (LOW - 1)) + HIGH).astype(jnp.bfloat16)
    digits = jnp.concatenate([high, low], axis=0)
    found = lax.dot_general(
        digits,
        part_ref[:, piece:],
        (((1,), (1,)), ((), ())),
        preferred_element_type=jnp.float32,
    )
    picks = found[:LANES] * found[LANES:]
    half = lax.broadcasted_iota(jnp.int32, picks.shape, 1) & SLOTS
    picks = jnp.concatenate(
        [jnp.where(half == 0, picks, 0.0), jnp.where(half == 0, 0.0, picks)], axis=0
    ).astype(jnp.bfloat16)
    sums = jnp.dot(picks, part_ref[...], preferred_element_type=jnp.float32)

    @pl.when(step == 0)
    def _():
        sum_ref[...] = sums

    @pl.when(step > 0)
    def _():
        sum_ref[...] += sums

    @pl.when(step == pl.num_programs(0) - 1)
    def _():
        out_ref[:, :piece] = sum_ref[:LANES, :piece].astype(jnp.bfloat16)
        out_ref[:, piece:] = sum_ref[LANES:, :piece].astype(jnp.bfloat16)


def collect(arrived):
    count, lanes = arrived.shape
    piece = lanes - CODE
    steps = 4
    return pl.pallas_call(
        collect_body,
        grid=(steps,),
        in_specs=[pl.BlockSpec((count // steps, lanes), lambda i: (i, 0))],
        out_specs=pl.BlockSpec((LANES, 2 * piece), lambda i: (0, 0)),
        out_shape=jax.ShapeDtypeStruct((LANES, 2 * piece), jnp.bfloat16),
        scratch_shapes=[pltpu.VMEM((2 * LANES, lanes), jnp.float32)],
        compiler_params=pltpu.CompilerParams(vmem_limit_bytes=40 * 1024 * 1024),
        cost_estimate=pl.CostEstimate(
            flops=2 * count * 2 * LANES * lanes,
            bytes_accessed=2 * (count * lanes + 2 * LANES * piece),
            transcendentals=0,
        ),
        name="collect",
    )(arrived)


def adam_body(rep_ref, sum_ref, table_ref, gain_ref, one_ref, two_ref, up_ref, rest_ref, one_out, two_out):
    width = table_ref.shape[1]
    root = math.sqrt(width)
    params = table_ref[...].astype(jnp.float32)
    scaled = params * root
    rows = table_ref.shape[0]
    totals = []
    for member in range(MEMBERS):
        total = sum_ref[member * rows : (member + 1) * rows, :].astype(jnp.float32)
        for peer in range(member + MEMBERS, sum_ref.shape[0] // rows, MEMBERS):
            total = total + sum_ref[peer * rows : (peer + 1) * rows, :].astype(jnp.float32)
        totals.append(total)
    weighted = jnp.concatenate(totals, axis=1) * gain_ref[...]
    mean_square = jnp.mean(scaled * scaled, axis=-1, keepdims=True)
    inverse = lax.rsqrt(mean_square + norm_eps)
    inner_mean = jnp.mean(scaled * weighted, axis=-1, keepdims=True)
    grad = root * inverse * (weighted - scaled * (inverse * inverse * inner_mean))
    new_one = beta_one * one_ref[...] + (1.0 - beta_one) * grad
    new_two = beta_two * two_ref[...] + (1.0 - beta_two) * grad * grad
    one_out[...] = new_one
    two_out[...] = new_two
    update = (
        new_one / correct_one / (jnp.sqrt(new_two / correct_two) + adam_eps) + decay_rate * params
    )
    updated = (params - learn_rate * update).astype(jnp.bfloat16)
    up_ref[...] = updated[:, :GATHERED]
    rest = updated[:, GATHERED:]
    for peer in range(rest_ref.shape[0] // rows):
        rest_ref[peer * rows : (peer + 1) * rows, :] = rest


def adam(rep_index, partial_sums, embed_table, norm_gain, moment_one, moment_two):
    rows, width = moment_one.shape
    peers = embed_table.shape[0] // rows
    whole = pl.BlockSpec((rows, width), lambda i, rep: (0, 0))
    return pl.pallas_call(
        adam_body,
        grid_spec=pltpu.PrefetchScalarGridSpec(
            num_scalar_prefetch=1,
            grid=(1,),
            in_specs=[
                pl.BlockSpec((peers * rows, width // MEMBERS), lambda i, rep: (0, 0)),
                pl.BlockSpec((rows, width), lambda i, rep: (rep[0], 0)),
                pl.BlockSpec((1, width), lambda i, rep: (0, 0)),
                whole,
                whole,
            ],
            out_specs=[
                pl.BlockSpec((rows, GATHERED), lambda i, rep: (0, 0)),
                pl.BlockSpec((peers * rows, width - GATHERED), lambda i, rep: (0, 0)),
                whole,
                whole,
            ],
        ),
        out_shape=[
            jax.ShapeDtypeStruct((rows, GATHERED), jnp.bfloat16),
            jax.ShapeDtypeStruct((peers * rows, width - GATHERED), jnp.bfloat16),
            jax.ShapeDtypeStruct((rows, width), jnp.float32),
            jax.ShapeDtypeStruct((rows, width), jnp.float32),
        ],
        compiler_params=pltpu.CompilerParams(vmem_limit_bytes=40 * 1024 * 1024),
        cost_estimate=pl.CostEstimate(
            flops=40 * rows * width, bytes_accessed=24 * rows * width, transcendentals=rows * width
        ),
        name="adam",
    )(rep_index, partial_sums, embed_table, norm_gain.reshape(1, width), moment_one, moment_two)


REP = ("two", "four")
ALL = ("vocab", "two", "four")


def on_device(token_ids, cotangent, embed_table, norm_gain, moment_one, moment_two):
    peer_count = lax.axis_size("vocab")
    outgoing = pack(token_ids, cotangent, peer_count)
    outgoing = outgoing.reshape(-1, outgoing.shape[-1])
    arrived = lax.all_to_all(outgoing, ("vocab", "four"), split_axis=0, concat_axis=0, tiled=True)
    row_sum = collect(arrived)
    partial_sums = lax.all_to_all(row_sum, REP, split_axis=0, concat_axis=0, tiled=True)
    rep_index = lax.axis_index(REP).astype(jnp.int32).reshape(1)
    updated, rest, new_moment_one, new_moment_two = adam(
        rep_index, partial_sums, embed_table, norm_gain, moment_one, moment_two
    )
    left = lax.all_gather(updated, REP, axis=0, tiled=True)
    right = lax.all_to_all(rest, REP, split_axis=0, concat_axis=0, tiled=True)
    new_table = jnp.concatenate([left, right], axis=1)
    return (new_table, new_moment_one, new_moment_two)


def solution(mesh):
    vocab, rep = mesh.devices.shape
    fours = Mesh(mesh.devices.reshape(vocab, rep // MEMBERS, MEMBERS), ALL)
    placed = (
        P(ALL),
        P(ALL, None),
        P("vocab", None),
        P(),
        P(ALL, None),
        P(ALL, None),
    )
    return jax.shard_map(
        on_device,
        mesh=fours,
        in_specs=placed,
        out_specs=(P("vocab", None), P(ALL, None), P(ALL, None)),
        check_vma=False,
    )
```

```python
import math

import jax
import jax.numpy as jnp
from jax import lax
from jax.experimental import pallas as pl
from jax.experimental.pallas import tpu as pltpu
from jax.sharding import Mesh
from jax.sharding import PartitionSpec as P

beta_one = 0.9
beta_two = 0.95
learn_rate = 0.01
decay_rate = 0.01
adam_eps = 1e-08
norm_eps = 1e-06
correct_one = 0.9999734386011124
correct_two = 0.9940794707920236

SLOTS = 4
LANES = 128
GATHERED = 3968
MEMBERS = 4
HIGH = 8
LOW = 16
CODE = 64
PACK_VMEM = 60 * 1024 * 1024


def pack_body(ids_hbm, cot_hbm, out_ref, ids_ref, cot_ref, piece_ref, slot_ref, sems):
    tok_count, width = cot_ref.shape
    piece = width // (2 * MEMBERS)
    lanes = out_ref.shape[-1]

    @pl.when(pl.program_id(0) == 0)
    def _():
        copy_ids = pltpu.make_async_copy(ids_hbm, ids_ref, sems.at[0])
        copy_cot = pltpu.make_async_copy(cot_hbm, cot_ref, sems.at[1])
        copy_ids.start()
        copy_cot.start()
        copy_ids.wait()
        ids_along = jnp.broadcast_to(ids_ref[...], (tok_count, tok_count))
        ids_down = ids_along.T
        down = lax.broadcasted_iota(jnp.int32, (tok_count, tok_count), 0)
        along = lax.broadcasted_iota(jnp.int32, (tok_count, tok_count), 1)
        earlier = ((ids_along >> 7) == (ids_down >> 7)) & (down < along)
        position = jnp.sum(earlier.astype(jnp.int32), axis=0, keepdims=True)
        slot_ref[...] = (ids_ref[...] >> 7) * (2 * SLOTS) + position
        high = (ids_down >> 4) & (HIGH - 1)
        low = (ids_down & (LOW - 1)) + 2 * HIGH
        marks = [
            ((along == high + half * HIGH) | (along == low)).astype(jnp.bfloat16)[:, : lanes - piece]
            for half in range(2)
        ]
        copy_cot.wait()
        for at in range(2 * MEMBERS):
            member, half = at // 2, at % 2
            rows = slice(half * tok_count, (half + 1) * tok_count)
            piece_ref[member, rows, :piece] = cot_ref[:, at * piece : (at + 1) * piece]
            piece_ref[member, rows, piece:] = marks[half]

    owners = out_ref.shape[0]
    block_rows = owners * 2 * SLOTS
    slots = jnp.concatenate([slot_ref[...], slot_ref[...] + SLOTS], axis=1)
    rows = lax.broadcasted_iota(jnp.int32, (block_rows, 2 * tok_count), 0)
    rows = rows + pl.program_id(0) * block_rows
    picks = (rows == slots).astype(jnp.bfloat16)
    for member in range(MEMBERS):
        moved = jnp.dot(picks, piece_ref[member], preferred_element_type=jnp.float32)
        out_ref[:, member] = moved.reshape(owners, 2 * SLOTS, lanes).astype(jnp.bfloat16)


def pack(token_ids, cotangent, peer_count):
    tok_count, width = cotangent.shape
    lanes = width // (2 * MEMBERS) + CODE
    steps = 4
    return pl.pallas_call(
        pack_body,
        grid=(steps,),
        in_specs=[pl.BlockSpec(memory_space=pl.ANY), pl.BlockSpec(memory_space=pl.ANY)],
        out_specs=pl.BlockSpec(
            (peer_count // steps, MEMBERS, 2 * SLOTS, lanes), lambda i: (i, 0, 0, 0)
        ),
        out_shape=jax.ShapeDtypeStruct((peer_count, MEMBERS, 2 * SLOTS, lanes), jnp.bfloat16),
        scratch_shapes=[
            pltpu.VMEM((1, tok_count), jnp.int32),
            pltpu.VMEM((tok_count, width), jnp.bfloat16),
            pltpu.VMEM((MEMBERS, 2 * tok_count, lanes), jnp.bfloat16),
            pltpu.VMEM((1, tok_count), jnp.int32),
            pltpu.SemaphoreType.DMA((2,)),
        ],
        compiler_params=pltpu.CompilerParams(vmem_limit_bytes=PACK_VMEM),
        cost_estimate=pl.CostEstimate(
            flops=2 * peer_count * 2 * SLOTS * 2 * tok_count * MEMBERS * lanes,
            bytes_accessed=2 * (tok_count * width + peer_count * MEMBERS * 2 * SLOTS * lanes),
            transcendentals=0,
        ),
        name="pack",
    )(token_ids.reshape(1, tok_count), cotangent)


def collect_body(part_ref, out_ref):
    piece = out_ref.shape[1] // 2
    shard_row = lax.broadcasted_iota(jnp.int32, (LANES, CODE), 0)
    lane = lax.broadcasted_iota(jnp.int32, (LANES, CODE), 1)
    high = shard_row >> 4
    low = (shard_row & (LOW - 1)) + 2 * HIGH
    digits = jnp.concatenate(
        [(lane == value).astype(jnp.bfloat16) for value in (high, high + HIGH, low)], axis=0
    )
    found = lax.dot_general(
        digits,
        part_ref[:, piece:],
        (((1,), (1,)), ((), ())),
        preferred_element_type=jnp.float32,
    )
    picks = (found[: 2 * LANES].reshape(2, LANES, -1) * found[2 * LANES :][None]).reshape(
        2 * LANES, -1
    )
    sums = jnp.dot(
        picks.astype(jnp.bfloat16), part_ref[...], preferred_element_type=jnp.float32
    ).astype(jnp.bfloat16)
    out_ref[:, :piece] = sums[:LANES, :piece]
    out_ref[:, piece:] = sums[LANES:, :piece]


def collect(arrived):
    count, lanes = arrived.shape
    piece = lanes - CODE
    return pl.pallas_call(
        collect_body,
        in_specs=[pl.BlockSpec(memory_space=pltpu.VMEM)],
        out_specs=pl.BlockSpec(memory_space=pltpu.VMEM),
        out_shape=jax.ShapeDtypeStruct((LANES, 2 * piece), jnp.bfloat16),
        compiler_params=pltpu.CompilerParams(vmem_limit_bytes=40 * 1024 * 1024),
        cost_estimate=pl.CostEstimate(
            flops=2 * count * 2 * LANES * lanes,
            bytes_accessed=2 * (count * lanes + 2 * LANES * piece),
            transcendentals=0,
        ),
        name="collect",
    )(arrived)


def adam_body(rep_ref, sum_ref, table_ref, gain_ref, one_ref, two_ref, up_ref, rest_ref, one_out, two_out):
    width = table_ref.shape[1]
    root = math.sqrt(width)
    params = table_ref[...].astype(jnp.float32)
    scaled = params * root
    rows = table_ref.shape[0]
    totals = []
    for member in range(MEMBERS):
        total = sum_ref[member * rows : (member + 1) * rows, :].astype(jnp.float32)
        for peer in range(member + MEMBERS, sum_ref.shape[0] // rows, MEMBERS):
            total = total + sum_ref[peer * rows : (peer + 1) * rows, :].astype(jnp.float32)
        totals.append(total)
    weighted = jnp.concatenate(totals, axis=1) * gain_ref[...]
    mean_square = jnp.mean(scaled * scaled, axis=-1, keepdims=True)
    inverse = lax.rsqrt(mean_square + norm_eps)
    inner_mean = jnp.mean(scaled * weighted, axis=-1, keepdims=True)
    grad = root * inverse * (weighted - scaled * (inverse * inverse * inner_mean))
    new_one = beta_one * one_ref[...] + (1.0 - beta_one) * grad
    new_two = beta_two * two_ref[...] + (1.0 - beta_two) * grad * grad
    one_out[...] = new_one
    two_out[...] = new_two
    update = (
        new_one / correct_one / (jnp.sqrt(new_two / correct_two) + adam_eps) + decay_rate * params
    )
    updated = (params - learn_rate * update).astype(jnp.bfloat16)
    up_ref[...] = updated[:, :GATHERED]
    rest = updated[:, GATHERED:]
    for peer in range(rest_ref.shape[0] // rows):
        rest_ref[peer * rows : (peer + 1) * rows, :] = rest


def adam(rep_index, partial_sums, embed_table, norm_gain, moment_one, moment_two):
    rows, width = moment_one.shape
    peers = embed_table.shape[0] // rows
    whole = pl.BlockSpec((rows, width), lambda i, rep: (0, 0))
    return pl.pallas_call(
        adam_body,
        grid_spec=pltpu.PrefetchScalarGridSpec(
            num_scalar_prefetch=1,
            grid=(1,),
            in_specs=[
                pl.BlockSpec((peers * rows, width // MEMBERS), lambda i, rep: (0, 0)),
                pl.BlockSpec((rows, width), lambda i, rep: (rep[0], 0)),
                pl.BlockSpec((1, width), lambda i, rep: (0, 0)),
                whole,
                whole,
            ],
            out_specs=[
                pl.BlockSpec((rows, GATHERED), lambda i, rep: (0, 0)),
                pl.BlockSpec((peers * rows, width - GATHERED), lambda i, rep: (0, 0)),
                whole,
                whole,
            ],
        ),
        out_shape=[
            jax.ShapeDtypeStruct((rows, GATHERED), jnp.bfloat16),
            jax.ShapeDtypeStruct((peers * rows, width - GATHERED), jnp.bfloat16),
            jax.ShapeDtypeStruct((rows, width), jnp.float32),
            jax.ShapeDtypeStruct((rows, width), jnp.float32),
        ],
        compiler_params=pltpu.CompilerParams(vmem_limit_bytes=40 * 1024 * 1024),
        cost_estimate=pl.CostEstimate(
            flops=40 * rows * width, bytes_accessed=24 * rows * width, transcendentals=rows * width
        ),
        name="adam",
    )(rep_index, partial_sums, embed_table, norm_gain.reshape(1, width), moment_one, moment_two)


REP = ("two", "four")
ALL = ("vocab", "two", "four")


def on_device(token_ids, cotangent, embed_table, norm_gain, moment_one, moment_two):
    peer_count = lax.axis_size("vocab")
    outgoing = pack(token_ids, cotangent, peer_count)
    outgoing = outgoing.reshape(-1, outgoing.shape[-1])
    arrived = lax.all_to_all(outgoing, ("vocab", "four"), split_axis=0, concat_axis=0, tiled=True)
    row_sum = collect(arrived)
    partial_sums = lax.all_to_all(row_sum, REP, split_axis=0, concat_axis=0, tiled=True)
    rep_index = lax.axis_index(REP).astype(jnp.int32).reshape(1)
    updated, rest, new_moment_one, new_moment_two = adam(
        rep_index, partial_sums, embed_table, norm_gain, moment_one, moment_two
    )
    left = lax.all_gather(updated, REP, axis=0, tiled=True)
    right = lax.all_to_all(rest, REP, split_axis=0, concat_axis=0, tiled=True)
    new_table = jnp.concatenate([left, right], axis=1)
    return (new_table, new_moment_one, new_moment_two)


def solution(mesh):
    vocab, rep = mesh.devices.shape
    fours = Mesh(mesh.devices.reshape(vocab, rep // MEMBERS, MEMBERS), ALL)
    placed = (
        P(ALL),
        P(ALL, None),
        P("vocab", None),
        P(),
        P(ALL, None),
        P(ALL, None),
    )
    return jax.shard_map(
        on_device,
        mesh=fours,
        in_specs=placed,
        out_specs=(P("vocab", None), P(ALL, None), P(ALL, None)),
        check_vma=False,
    )
```

```python
import math

import jax
import jax.numpy as jnp
from jax import lax
from jax.experimental import pallas as pl
from jax.experimental.pallas import tpu as pltpu
from jax.sharding import Mesh
from jax.sharding import PartitionSpec as P

beta_one = 0.9
beta_two = 0.95
learn_rate = 0.01
decay_rate = 0.01
adam_eps = 1e-08
norm_eps = 1e-06
correct_one = 0.9999734386011124
correct_two = 0.9940794707920236

SLOTS = 4
LANES = 128
GATHERED = 3968
MEMBERS = 4
HIGH = 8
LOW = 16
CODE = 64


def pack_body(ids_hbm, cot_hbm, out_hbm, ids_ref, cot_ref, piece_ref, out_ref, sems, out_sems):
    tok_count, width = cot_ref.shape
    own = width // MEMBERS
    piece = own // 2
    _, owners, per_owner, lanes = out_ref.shape
    copy_ids = pltpu.make_async_copy(ids_hbm, ids_ref, sems.at[MEMBERS])
    copies = [
        pltpu.make_async_copy(
            cot_hbm.at[:, member * own : (member + 1) * own],
            cot_ref.at[:, member * own : (member + 1) * own],
            sems.at[member],
        )
        for member in range(MEMBERS)
    ]
    copy_ids.start()
    for copy in copies:
        copy.start()
    copy_ids.wait()
    ids_along = jnp.broadcast_to(ids_ref[...], (tok_count, tok_count))
    ids_down = ids_along.T
    down = lax.broadcasted_iota(jnp.int32, (tok_count, tok_count), 0)
    along = lax.broadcasted_iota(jnp.int32, (tok_count, tok_count), 1)
    earlier = ((ids_along >> 7) == (ids_down >> 7)) & (down < along)
    position = jnp.sum(earlier.astype(jnp.int32), axis=0, keepdims=True)
    slot = (ids_ref[...] >> 7) * per_owner + position
    slots = jnp.concatenate([slot, slot + SLOTS], axis=1)
    rows = lax.broadcasted_iota(jnp.int32, (owners * per_owner, 2 * tok_count), 0)
    picks = (rows == slots).astype(jnp.bfloat16)
    high = (ids_down >> 4) & (HIGH - 1)
    low = (ids_down & (LOW - 1)) + 2 * HIGH
    marks = [
        ((along == high + half * HIGH) | (along == low)).astype(jnp.bfloat16)[:, : lanes - piece]
        for half in range(2)
    ]
    for member in range(MEMBERS):
        for half in range(2):
            piece_ref[member, half * tok_count : (half + 1) * tok_count, piece:] = marks[half]
    sends = []
    for member in range(MEMBERS):
        copies[member].wait()
        for half in range(2):
            at = member * own + half * piece
            piece_ref[member, half * tok_count : (half + 1) * tok_count, :piece] = cot_ref[
                :, at : at + piece
            ]
        moved = jnp.dot(picks, piece_ref[member], preferred_element_type=jnp.float32)
        out_ref[member] = moved.reshape(owners, per_owner, lanes).astype(jnp.bfloat16)
        sends.append(
            pltpu.make_async_copy(out_ref.at[member], out_hbm.at[:, member], out_sems.at[member])
        )
        sends[member].start()
    for send in sends:
        send.wait()


def pack(token_ids, cotangent, peer_count):
    tok_count, width = cotangent.shape
    lanes = width // (2 * MEMBERS) + CODE
    return pl.pallas_call(
        pack_body,
        in_specs=[pl.BlockSpec(memory_space=pl.ANY), pl.BlockSpec(memory_space=pl.ANY)],
        out_specs=pl.BlockSpec(memory_space=pl.ANY),
        out_shape=jax.ShapeDtypeStruct((peer_count, MEMBERS, 2 * SLOTS, lanes), jnp.bfloat16),
        scratch_shapes=[
            pltpu.VMEM((1, tok_count), jnp.int32),
            pltpu.VMEM((tok_count, width), jnp.bfloat16),
            pltpu.VMEM((MEMBERS, 2 * tok_count, lanes), jnp.bfloat16),
            pltpu.VMEM((MEMBERS, peer_count, 2 * SLOTS, lanes), jnp.bfloat16),
            pltpu.SemaphoreType.DMA((MEMBERS + 1,)),
            pltpu.SemaphoreType.DMA((MEMBERS,)),
        ],
        compiler_params=pltpu.CompilerParams(vmem_limit_bytes=58 * 1024 * 1024),
        cost_estimate=pl.CostEstimate(
            flops=2 * peer_count * 2 * SLOTS * 2 * tok_count * MEMBERS * lanes,
            bytes_accessed=2 * (tok_count * width + peer_count * MEMBERS * 2 * SLOTS * lanes),
            transcendentals=0,
        ),
        name="pack",
    )(token_ids.reshape(1, tok_count), cotangent)


def collect_body(part_ref, out_ref):
    piece = out_ref.shape[1] // 2
    shard_row = lax.broadcasted_iota(jnp.int32, (LANES, CODE), 0)
    lane = lax.broadcasted_iota(jnp.int32, (LANES, CODE), 1)
    high = shard_row >> 4
    low = (shard_row & (LOW - 1)) + 2 * HIGH
    digits = jnp.concatenate(
        [(lane == value).astype(jnp.bfloat16) for value in (high, high + HIGH, low)], axis=0
    )
    found = lax.dot_general(
        digits,
        part_ref[:, piece:],
        (((1,), (1,)), ((), ())),
        preferred_element_type=jnp.float32,
    )
    picks = (found[: 2 * LANES].reshape(2, LANES, -1) * found[2 * LANES :][None]).reshape(
        2 * LANES, -1
    )
    sums = jnp.dot(
        picks.astype(jnp.bfloat16), part_ref[...], preferred_element_type=jnp.float32
    ).astype(jnp.bfloat16)
    out_ref[:, :piece] = sums[:LANES, :piece]
    out_ref[:, piece:] = sums[LANES:, :piece]


def collect(arrived):
    count, lanes = arrived.shape
    piece = lanes - CODE
    return pl.pallas_call(
        collect_body,
        in_specs=[pl.BlockSpec(memory_space=pltpu.VMEM)],
        out_specs=pl.BlockSpec(memory_space=pltpu.VMEM),
        out_shape=jax.ShapeDtypeStruct((LANES, 2 * piece), jnp.bfloat16),
        compiler_params=pltpu.CompilerParams(vmem_limit_bytes=40 * 1024 * 1024),
        cost_estimate=pl.CostEstimate(
            flops=2 * count * 2 * LANES * lanes,
            bytes_accessed=2 * (count * lanes + 2 * LANES * piece),
            transcendentals=0,
        ),
        name="collect",
    )(arrived)


def adam_body(rep_ref, sum_ref, table_ref, gain_ref, one_ref, two_ref, up_ref, rest_ref, one_out, two_out):
    width = table_ref.shape[1]
    root = math.sqrt(width)
    params = table_ref[...].astype(jnp.float32)
    scaled = params * root
    rows = table_ref.shape[0]
    totals = []
    for member in range(MEMBERS):
        total = sum_ref[member * rows : (member + 1) * rows, :].astype(jnp.float32)
        for peer in range(member + MEMBERS, sum_ref.shape[0] // rows, MEMBERS):
            total = total + sum_ref[peer * rows : (peer + 1) * rows, :].astype(jnp.float32)
        totals.append(total)
    weighted = jnp.concatenate(totals, axis=1) * gain_ref[...]
    mean_square = jnp.mean(scaled * scaled, axis=-1, keepdims=True)
    inverse = lax.rsqrt(mean_square + norm_eps)
    inner_mean = jnp.mean(scaled * weighted, axis=-1, keepdims=True)
    grad = root * inverse * (weighted - scaled * (inverse * inverse * inner_mean))
    new_one = beta_one * one_ref[...] + (1.0 - beta_one) * grad
    new_two = beta_two * two_ref[...] + (1.0 - beta_two) * grad * grad
    one_out[...] = new_one
    two_out[...] = new_two
    update = (
        new_one / correct_one / (jnp.sqrt(new_two / correct_two) + adam_eps) + decay_rate * params
    )
    updated = (params - learn_rate * update).astype(jnp.bfloat16)
    up_ref[...] = updated[:, :GATHERED]
    rest = updated[:, GATHERED:]
    for peer in range(rest_ref.shape[0] // rows):
        rest_ref[peer * rows : (peer + 1) * rows, :] = rest


def adam(rep_index, partial_sums, embed_table, norm_gain, moment_one, moment_two):
    rows, width = moment_one.shape
    peers = embed_table.shape[0] // rows
    whole = pl.BlockSpec((rows, width), lambda i, rep: (0, 0))
    return pl.pallas_call(
        adam_body,
        grid_spec=pltpu.PrefetchScalarGridSpec(
            num_scalar_prefetch=1,
            grid=(1,),
            in_specs=[
                pl.BlockSpec((peers * rows, width // MEMBERS), lambda i, rep: (0, 0)),
                pl.BlockSpec((rows, width), lambda i, rep: (rep[0], 0)),
                pl.BlockSpec((1, width), lambda i, rep: (0, 0)),
                whole,
                whole,
            ],
            out_specs=[
                pl.BlockSpec((rows, GATHERED), lambda i, rep: (0, 0)),
                pl.BlockSpec((peers * rows, width - GATHERED), lambda i, rep: (0, 0)),
                whole,
                whole,
            ],
        ),
        out_shape=[
            jax.ShapeDtypeStruct((rows, GATHERED), jnp.bfloat16),
            jax.ShapeDtypeStruct((peers * rows, width - GATHERED), jnp.bfloat16),
            jax.ShapeDtypeStruct((rows, width), jnp.float32),
            jax.ShapeDtypeStruct((rows, width), jnp.float32),
        ],
        compiler_params=pltpu.CompilerParams(vmem_limit_bytes=40 * 1024 * 1024),
        cost_estimate=pl.CostEstimate(
            flops=40 * rows * width, bytes_accessed=24 * rows * width, transcendentals=rows * width
        ),
        name="adam",
    )(rep_index, partial_sums, embed_table, norm_gain.reshape(1, width), moment_one, moment_two)


REP = ("two", "four")
ALL = ("vocab", "two", "four")


def on_device(token_ids, cotangent, embed_table, norm_gain, moment_one, moment_two):
    peer_count = lax.axis_size("vocab")
    outgoing = pack(token_ids, cotangent, peer_count)
    outgoing = outgoing.reshape(-1, outgoing.shape[-1])
    arrived = lax.all_to_all(outgoing, ("vocab", "four"), split_axis=0, concat_axis=0, tiled=True)
    row_sum = collect(arrived)
    partial_sums = lax.all_to_all(row_sum, REP, split_axis=0, concat_axis=0, tiled=True)
    rep_index = lax.axis_index(REP).astype(jnp.int32).reshape(1)
    updated, rest, new_moment_one, new_moment_two = adam(
        rep_index, partial_sums, embed_table, norm_gain, moment_one, moment_two
    )
    left = lax.all_gather(updated, REP, axis=0, tiled=True)
    right = lax.all_to_all(rest, REP, split_axis=0, concat_axis=0, tiled=True)
    new_table = jnp.concatenate([left, right], axis=1)
    return (new_table, new_moment_one, new_moment_two)


def solution(mesh):
    vocab, rep = mesh.devices.shape
    fours = Mesh(mesh.devices.reshape(vocab, rep // MEMBERS, MEMBERS), ALL)
    placed = (
        P(ALL),
        P(ALL, None),
        P("vocab", None),
        P(),
        P(ALL, None),
        P(ALL, None),
    )
    return jax.shard_map(
        on_device,
        mesh=fours,
        in_specs=placed,
        out_specs=(P("vocab", None), P(ALL, None), P(ALL, None)),
        check_vma=False,
    )
```

```python
import math

import jax
import jax.numpy as jnp
from jax import lax
from jax.experimental import pallas as pl
from jax.experimental.pallas import tpu as pltpu
from jax.sharding import Mesh
from jax.sharding import PartitionSpec as P

beta_one = 0.9
beta_two = 0.95
learn_rate = 0.01
decay_rate = 0.01
adam_eps = 1e-08
norm_eps = 1e-06
correct_one = 0.9999734386011124
correct_two = 0.9940794707920236

SLOTS = 4
LANES = 128
GATHERED = 3968
MEMBERS = 4
HIGH = 8
LOW = 16
CODE = 64


def pack_body(ids_hbm, cot_hbm, out_hbm, ids_ref, cot_ref, piece_ref, out_ref, sems, out_sems):
    tok_count, width = cot_ref.shape
    own = width // MEMBERS
    piece = own // 2
    _, owners, per_owner, lanes = out_ref.shape
    copy_ids = pltpu.make_async_copy(ids_hbm, ids_ref, sems.at[MEMBERS])
    copies = [
        pltpu.make_async_copy(
            cot_hbm.at[:, member * own : (member + 1) * own],
            cot_ref.at[:, member * own : (member + 1) * own],
            sems.at[member],
        )
        for member in range(MEMBERS)
    ]
    copy_ids.start()
    for copy in copies:
        copy.start()
    copy_ids.wait()
    ids_along = jnp.broadcast_to(ids_ref[...], (tok_count, tok_count))
    ids_down = ids_along.T
    down = lax.broadcasted_iota(jnp.int32, (tok_count, tok_count), 0)
    along = lax.broadcasted_iota(jnp.int32, (tok_count, tok_count), 1)
    earlier = ((ids_along >> 7) == (ids_down >> 7)) & (down < along)
    position = jnp.sum(earlier.astype(jnp.int32), axis=0, keepdims=True)
    slot = (ids_ref[...] >> 7) * per_owner + position
    slots = jnp.concatenate([slot, slot + SLOTS], axis=1)
    rows = lax.broadcasted_iota(jnp.int32, (owners * per_owner, 2 * tok_count), 0)
    picks = (rows == slots).astype(jnp.bfloat16)
    high = (ids_down >> 4) & (HIGH - 1)
    low = (ids_down & (LOW - 1)) + 2 * HIGH
    marks = [
        ((along == high + half * HIGH) | (along == low)).astype(jnp.bfloat16)[:, : lanes - piece]
        for half in range(2)
    ]
    for member in range(MEMBERS):
        for half in range(2):
            piece_ref[member, half * tok_count : (half + 1) * tok_count, piece:] = marks[half]
    sends = []
    for member in range(MEMBERS):
        copies[member].wait()
        for half in range(2):
            at = member * own + half * piece
            piece_ref[member, half * tok_count : (half + 1) * tok_count, :piece] = cot_ref[
                :, at : at + piece
            ]
        moved = jnp.dot(picks, piece_ref[member], preferred_element_type=jnp.float32)
        out_ref[member] = moved.reshape(owners, per_owner, lanes).astype(jnp.bfloat16)
        sends.append(
            pltpu.make_async_copy(out_ref.at[member], out_hbm.at[:, member], out_sems.at[member])
        )
        sends[member].start()
    for send in sends:
        send.wait()


def pack(token_ids, cotangent, peer_count):
    tok_count, width = cotangent.shape
    lanes = width // (2 * MEMBERS) + CODE
    return pl.pallas_call(
        pack_body,
        in_specs=[pl.BlockSpec(memory_space=pl.ANY), pl.BlockSpec(memory_space=pl.ANY)],
        out_specs=pl.BlockSpec(memory_space=pl.ANY),
        out_shape=jax.ShapeDtypeStruct((peer_count, MEMBERS, 2 * SLOTS, lanes), jnp.bfloat16),
        scratch_shapes=[
            pltpu.VMEM((1, tok_count), jnp.int32),
            pltpu.VMEM((tok_count, width), jnp.bfloat16),
            pltpu.VMEM((MEMBERS, 2 * tok_count, lanes), jnp.bfloat16),
            pltpu.VMEM((MEMBERS, peer_count, 2 * SLOTS, lanes), jnp.bfloat16),
            pltpu.SemaphoreType.DMA((MEMBERS + 1,)),
            pltpu.SemaphoreType.DMA((MEMBERS,)),
        ],
        compiler_params=pltpu.CompilerParams(vmem_limit_bytes=58 * 1024 * 1024),
        cost_estimate=pl.CostEstimate(
            flops=2 * peer_count * 2 * SLOTS * 2 * tok_count * MEMBERS * lanes,
            bytes_accessed=2 * (tok_count * width + peer_count * MEMBERS * 2 * SLOTS * lanes),
            transcendentals=0,
        ),
        name="pack",
    )(token_ids.reshape(1, tok_count), cotangent)


def collect_body(part_ref, out_ref):
    piece = out_ref.shape[1] // 2
    shard_row = lax.broadcasted_iota(jnp.int32, (LANES, CODE), 0)
    lane = lax.broadcasted_iota(jnp.int32, (LANES, CODE), 1)
    high = shard_row >> 4
    low = (shard_row & (LOW - 1)) + 2 * HIGH
    digits = jnp.concatenate(
        [(lane == value).astype(jnp.bfloat16) for value in (high, high + HIGH, low)], axis=0
    )
    found = lax.dot_general(
        digits,
        part_ref[:, piece:],
        (((1,), (1,)), ((), ())),
        preferred_element_type=jnp.float32,
    )
    picks = (found[: 2 * LANES].reshape(2, LANES, -1) * found[2 * LANES :][None]).reshape(
        2 * LANES, -1
    )
    sums = jnp.dot(picks.astype(jnp.bfloat16), part_ref[...], preferred_element_type=jnp.float32)
    out_ref[:, :piece] = sums[:LANES, :piece]
    out_ref[:, piece:] = sums[LANES:, :piece]


def collect(arrived):
    count, lanes = arrived.shape
    piece = lanes - CODE
    return pl.pallas_call(
        collect_body,
        in_specs=[pl.BlockSpec(memory_space=pltpu.VMEM)],
        out_specs=pl.BlockSpec(memory_space=pltpu.VMEM),
        out_shape=jax.ShapeDtypeStruct((LANES, 2 * piece), jnp.float32),
        compiler_params=pltpu.CompilerParams(vmem_limit_bytes=40 * 1024 * 1024),
        cost_estimate=pl.CostEstimate(
            flops=2 * count * 2 * LANES * lanes,
            bytes_accessed=2 * count * lanes + 8 * LANES * piece,
            transcendentals=0,
        ),
        name="collect",
    )(arrived)


def adam_body(rep_ref, sum_ref, table_ref, gain_ref, one_ref, two_ref, up_ref, rest_ref, one_out, two_out):
    width = table_ref.shape[1]
    root = math.sqrt(width)
    params = table_ref[...].astype(jnp.float32)
    scaled = params * root
    rows = table_ref.shape[0]
    totals = []
    for member in range(MEMBERS):
        total = sum_ref[member * rows : (member + 1) * rows, :]
        for peer in range(member + MEMBERS, sum_ref.shape[0] // rows, MEMBERS):
            total = total + sum_ref[peer * rows : (peer + 1) * rows, :]
        totals.append(total)
    weighted = jnp.concatenate(totals, axis=1) * gain_ref[...]
    mean_square = jnp.mean(scaled * scaled, axis=-1, keepdims=True)
    inverse = lax.rsqrt(mean_square + norm_eps)
    inner_mean = jnp.mean(scaled * weighted, axis=-1, keepdims=True)
    grad = root * inverse * (weighted - scaled * (inverse * inverse * inner_mean))
    new_one = beta_one * one_ref[...] + (1.0 - beta_one) * grad
    new_two = beta_two * two_ref[...] + (1.0 - beta_two) * grad * grad
    one_out[...] = new_one
    two_out[...] = new_two
    update = (
        new_one / correct_one / (jnp.sqrt(new_two / correct_two) + adam_eps) + decay_rate * params
    )
    updated = (params - learn_rate * update).astype(jnp.bfloat16)
    up_ref[...] = updated[:, :GATHERED]
    rest = updated[:, GATHERED:]
    for peer in range(rest_ref.shape[0] // rows):
        rest_ref[peer * rows : (peer + 1) * rows, :] = rest


def adam(rep_index, partial_sums, embed_table, norm_gain, moment_one, moment_two):
    rows, width = moment_one.shape
    peers = embed_table.shape[0] // rows
    whole = pl.BlockSpec((rows, width), lambda i, rep: (0, 0))
    return pl.pallas_call(
        adam_body,
        grid_spec=pltpu.PrefetchScalarGridSpec(
            num_scalar_prefetch=1,
            grid=(1,),
            in_specs=[
                pl.BlockSpec((peers * rows, width // MEMBERS), lambda i, rep: (0, 0)),
                pl.BlockSpec((rows, width), lambda i, rep: (rep[0], 0)),
                pl.BlockSpec((1, width), lambda i, rep: (0, 0)),
                whole,
                whole,
            ],
            out_specs=[
                pl.BlockSpec((rows, GATHERED), lambda i, rep: (0, 0)),
                pl.BlockSpec((peers * rows, width - GATHERED), lambda i, rep: (0, 0)),
                whole,
                whole,
            ],
        ),
        out_shape=[
            jax.ShapeDtypeStruct((rows, GATHERED), jnp.bfloat16),
            jax.ShapeDtypeStruct((peers * rows, width - GATHERED), jnp.bfloat16),
            jax.ShapeDtypeStruct((rows, width), jnp.float32),
            jax.ShapeDtypeStruct((rows, width), jnp.float32),
        ],
        compiler_params=pltpu.CompilerParams(vmem_limit_bytes=40 * 1024 * 1024),
        cost_estimate=pl.CostEstimate(
            flops=40 * rows * width, bytes_accessed=24 * rows * width, transcendentals=rows * width
        ),
        name="adam",
    )(rep_index, partial_sums, embed_table, norm_gain.reshape(1, width), moment_one, moment_two)


REP = ("two", "four")
ALL = ("vocab", "two", "four")


def on_device(token_ids, cotangent, embed_table, norm_gain, moment_one, moment_two):
    peer_count = lax.axis_size("vocab")
    outgoing = pack(token_ids, cotangent, peer_count)
    outgoing = outgoing.reshape(-1, outgoing.shape[-1])
    arrived = lax.all_to_all(outgoing, ("vocab", "four"), split_axis=0, concat_axis=0, tiled=True)
    row_sum = collect(arrived)
    partial_sums = lax.all_to_all(row_sum, REP, split_axis=0, concat_axis=0, tiled=True)
    rep_index = lax.axis_index(REP).astype(jnp.int32).reshape(1)
    updated, rest, new_moment_one, new_moment_two = adam(
        rep_index, partial_sums, embed_table, norm_gain, moment_one, moment_two
    )
    left = lax.all_gather(updated, REP, axis=0, tiled=True)
    right = lax.all_to_all(rest, REP, split_axis=0, concat_axis=0, tiled=True)
    new_table = jnp.concatenate([left, right], axis=1)
    return (new_table, new_moment_one, new_moment_two)


def solution(mesh):
    vocab, rep = mesh.devices.shape
    fours = Mesh(mesh.devices.reshape(vocab, rep // MEMBERS, MEMBERS), ALL)
    placed = (
        P(ALL),
        P(ALL, None),
        P("vocab", None),
        P(),
        P(ALL, None),
        P(ALL, None),
    )
    return jax.shard_map(
        on_device,
        mesh=fours,
        in_specs=placed,
        out_specs=(P("vocab", None), P(ALL, None), P(ALL, None)),
        check_vma=False,
    )
```

```python
import math

import jax
import jax.numpy as jnp
from jax import lax
from jax.experimental import pallas as pl
from jax.experimental.pallas import tpu as pltpu
from jax.sharding import Mesh
from jax.sharding import PartitionSpec as P

beta_one = 0.9
beta_two = 0.95
learn_rate = 0.01
decay_rate = 0.01
adam_eps = 1e-08
norm_eps = 1e-06
correct_one = 0.9999734386011124
correct_two = 0.9940794707920236

SLOTS = 4
LANES = 128
MEMBERS = 4
HIGH = 8
LOW = 16
CODE = 64


def pack_body(ids_hbm, cot_hbm, out_hbm, ids_ref, cot_ref, piece_ref, out_ref, sems, out_sems):
    tok_count, width = cot_ref.shape
    own = width // MEMBERS
    piece = own // 2
    _, owners, per_owner, lanes = out_ref.shape
    copy_ids = pltpu.make_async_copy(ids_hbm, ids_ref, sems.at[MEMBERS])
    copies = [
        pltpu.make_async_copy(
            cot_hbm.at[:, member * own : (member + 1) * own],
            cot_ref.at[:, member * own : (member + 1) * own],
            sems.at[member],
        )
        for member in range(MEMBERS)
    ]
    copy_ids.start()
    for copy in copies:
        copy.start()
    copy_ids.wait()
    ids_along = jnp.broadcast_to(ids_ref[...], (tok_count, tok_count))
    ids_down = ids_along.T
    down = lax.broadcasted_iota(jnp.int32, (tok_count, tok_count), 0)
    along = lax.broadcasted_iota(jnp.int32, (tok_count, tok_count), 1)
    earlier = ((ids_along >> 7) == (ids_down >> 7)) & (down < along)
    position = jnp.sum(earlier.astype(jnp.int32), axis=0, keepdims=True)
    slot = (ids_ref[...] >> 7) * per_owner + position
    slots = jnp.concatenate([slot, slot + SLOTS], axis=1)
    rows = lax.broadcasted_iota(jnp.int32, (owners * per_owner, 2 * tok_count), 0)
    picks = (rows == slots).astype(jnp.bfloat16)
    high = (ids_down >> 4) & (HIGH - 1)
    low = (ids_down & (LOW - 1)) + 2 * HIGH
    marks = [
        ((along == high + half * HIGH) | (along == low)).astype(jnp.bfloat16)[:, : lanes - piece]
        for half in range(2)
    ]
    for member in range(MEMBERS):
        for half in range(2):
            piece_ref[member, half * tok_count : (half + 1) * tok_count, piece:] = marks[half]
    sends = []
    for member in range(MEMBERS):
        copies[member].wait()
        for half in range(2):
            at = member * own + half * piece
            piece_ref[member, half * tok_count : (half + 1) * tok_count, :piece] = cot_ref[
                :, at : at + piece
            ]
        moved = jnp.dot(picks, piece_ref[member], preferred_element_type=jnp.float32)
        out_ref[member] = moved.reshape(owners, per_owner, lanes).astype(jnp.bfloat16)
        sends.append(
            pltpu.make_async_copy(out_ref.at[member], out_hbm.at[:, member], out_sems.at[member])
        )
        sends[member].start()
    for send in sends:
        send.wait()


def pack(token_ids, cotangent, peer_count):
    tok_count, width = cotangent.shape
    lanes = width // (2 * MEMBERS) + CODE
    return pl.pallas_call(
        pack_body,
        in_specs=[pl.BlockSpec(memory_space=pl.ANY), pl.BlockSpec(memory_space=pl.ANY)],
        out_specs=pl.BlockSpec(memory_space=pl.ANY),
        out_shape=jax.ShapeDtypeStruct((peer_count, MEMBERS, 2 * SLOTS, lanes), jnp.bfloat16),
        scratch_shapes=[
            pltpu.VMEM((1, tok_count), jnp.int32),
            pltpu.VMEM((tok_count, width), jnp.bfloat16),
            pltpu.VMEM((MEMBERS, 2 * tok_count, lanes), jnp.bfloat16),
            pltpu.VMEM((MEMBERS, peer_count, 2 * SLOTS, lanes), jnp.bfloat16),
            pltpu.SemaphoreType.DMA((MEMBERS + 1,)),
            pltpu.SemaphoreType.DMA((MEMBERS,)),
        ],
        compiler_params=pltpu.CompilerParams(vmem_limit_bytes=58 * 1024 * 1024),
        cost_estimate=pl.CostEstimate(
            flops=2 * peer_count * 2 * SLOTS * 2 * tok_count * MEMBERS * lanes,
            bytes_accessed=2 * (tok_count * width + peer_count * MEMBERS * 2 * SLOTS * lanes),
            transcendentals=0,
        ),
        name="pack",
    )(token_ids.reshape(1, tok_count), cotangent)


def collect_body(part_ref, out_ref):
    piece = out_ref.shape[1] // 2
    shard_row = lax.broadcasted_iota(jnp.int32, (LANES, CODE), 0)
    lane = lax.broadcasted_iota(jnp.int32, (LANES, CODE), 1)
    high = shard_row >> 4
    low = (shard_row & (LOW - 1)) + 2 * HIGH
    digits = jnp.concatenate(
        [(lane == value).astype(jnp.bfloat16) for value in (high, high + HIGH, low)], axis=0
    )
    found = lax.dot_general(
        digits,
        part_ref[:, piece:],
        (((1,), (1,)), ((), ())),
        preferred_element_type=jnp.float32,
    )
    picks = (found[: 2 * LANES].reshape(2, LANES, -1) * found[2 * LANES :][None]).reshape(
        2 * LANES, -1
    )
    sums = jnp.dot(
        picks.astype(jnp.bfloat16), part_ref[...], preferred_element_type=jnp.float32
    ).astype(jnp.bfloat16)
    out_ref[:, :piece] = sums[:LANES, :piece]
    out_ref[:, piece:] = sums[LANES:, :piece]


def collect(arrived):
    count, lanes = arrived.shape
    piece = lanes - CODE
    return pl.pallas_call(
        collect_body,
        in_specs=[pl.BlockSpec(memory_space=pltpu.VMEM)],
        out_specs=pl.BlockSpec(memory_space=pltpu.VMEM),
        out_shape=jax.ShapeDtypeStruct((LANES, 2 * piece), jnp.bfloat16),
        compiler_params=pltpu.CompilerParams(vmem_limit_bytes=40 * 1024 * 1024),
        cost_estimate=pl.CostEstimate(
            flops=2 * count * 2 * LANES * lanes,
            bytes_accessed=2 * (count * lanes + 2 * LANES * piece),
            transcendentals=0,
        ),
        name="collect",
    )(arrived)


def adam_body(rep_ref, sum_ref, table_ref, gain_ref, one_ref, two_ref, up_ref, one_out, two_out):
    width = table_ref.shape[1]
    root = math.sqrt(width)
    params = table_ref[...].astype(jnp.float32)
    scaled = params * root
    rows = table_ref.shape[0]
    totals = []
    for member in range(MEMBERS):
        total = sum_ref[member * rows : (member + 1) * rows, :].astype(jnp.float32)
        for peer in range(member + MEMBERS, sum_ref.shape[0] // rows, MEMBERS):
            total = total + sum_ref[peer * rows : (peer + 1) * rows, :].astype(jnp.float32)
        totals.append(total)
    weighted = jnp.concatenate(totals, axis=1) * gain_ref[...]
    mean_square = jnp.mean(scaled * scaled, axis=-1, keepdims=True)
    inverse = lax.rsqrt(mean_square + norm_eps)
    inner_mean = jnp.mean(scaled * weighted, axis=-1, keepdims=True)
    grad = root * inverse * (weighted - scaled * (inverse * inverse * inner_mean))
    new_one = beta_one * one_ref[...] + (1.0 - beta_one) * grad
    new_two = beta_two * two_ref[...] + (1.0 - beta_two) * grad * grad
    one_out[...] = new_one
    two_out[...] = new_two
    update = (
        new_one / correct_one / (jnp.sqrt(new_two / correct_two) + adam_eps) + decay_rate * params
    )
    up_ref[...] = (params - learn_rate * update).astype(jnp.bfloat16)


def adam(rep_index, partial_sums, embed_table, norm_gain, moment_one, moment_two):
    rows, width = moment_one.shape
    peers = embed_table.shape[0] // rows
    whole = pl.BlockSpec((rows, width), lambda i, rep: (0, 0))
    return pl.pallas_call(
        adam_body,
        grid_spec=pltpu.PrefetchScalarGridSpec(
            num_scalar_prefetch=1,
            grid=(1,),
            in_specs=[
                pl.BlockSpec((peers * rows, width // MEMBERS), lambda i, rep: (0, 0)),
                pl.BlockSpec((rows, width), lambda i, rep: (rep[0], 0)),
                pl.BlockSpec((1, width), lambda i, rep: (0, 0)),
                whole,
                whole,
            ],
            out_specs=[whole, whole, whole],
        ),
        out_shape=[
            jax.ShapeDtypeStruct((rows, width), jnp.bfloat16),
            jax.ShapeDtypeStruct((rows, width), jnp.float32),
            jax.ShapeDtypeStruct((rows, width), jnp.float32),
        ],
        compiler_params=pltpu.CompilerParams(vmem_limit_bytes=40 * 1024 * 1024),
        cost_estimate=pl.CostEstimate(
            flops=40 * rows * width, bytes_accessed=24 * rows * width, transcendentals=rows * width
        ),
        name="adam",
    )(rep_index, partial_sums, embed_table, norm_gain.reshape(1, width), moment_one, moment_two)


def place_body(side_ref, mine_ref, others_ref, out_hbm, sems):
    count, rows, _ = mine_ref.shape
    side = side_ref[0]
    copies = []
    for at in range(count):
        for which, source in enumerate((mine_ref, others_ref)):
            parity = side if which == 0 else 1 - side
            start = pl.multiple_of((2 * at + parity) * rows, rows)
            copies.append(
                pltpu.make_async_copy(
                    source.at[at], out_hbm.at[pl.ds(start, rows), :], sems.at[2 * at + which]
                )
            )
    for copy in copies:
        copy.start()
    for copy in copies:
        copy.wait()


def place(side, mine, others):
    count, rows, width = mine.shape
    return pl.pallas_call(
        place_body,
        in_specs=[
            pl.BlockSpec(memory_space=pltpu.SMEM),
            pl.BlockSpec(memory_space=pltpu.VMEM),
            pl.BlockSpec(memory_space=pltpu.VMEM),
        ],
        out_specs=pl.BlockSpec(memory_space=pl.ANY),
        out_shape=jax.ShapeDtypeStruct((2 * count * rows, width), mine.dtype),
        scratch_shapes=[pltpu.SemaphoreType.DMA((2 * count,))],
        compiler_params=pltpu.CompilerParams(vmem_limit_bytes=24 * 1024 * 1024),
        cost_estimate=pl.CostEstimate(
            flops=0, bytes_accessed=8 * count * rows * width, transcendentals=0
        ),
        name="place",
    )(side, mine, others)


REP = ("far", "near", "side")
ALL = ("vocab", "far", "near", "side")


def on_device(token_ids, cotangent, embed_table, norm_gain, moment_one, moment_two):
    peer_count = lax.axis_size("vocab")
    outgoing = pack(token_ids, cotangent, peer_count)
    outgoing = outgoing.reshape(-1, outgoing.shape[-1])
    arrived = lax.all_to_all(outgoing, ("vocab", "near", "side"), split_axis=0, concat_axis=0, tiled=True)
    row_sum = collect(arrived)
    partial_sums = lax.all_to_all(row_sum, REP, split_axis=0, concat_axis=0, tiled=True)
    rep_index = lax.axis_index(REP).astype(jnp.int32).reshape(1)
    updated, new_moment_one, new_moment_two = adam(
        rep_index, partial_sums, embed_table, norm_gain, moment_one, moment_two
    )
    mine = lax.all_gather(updated, ("far", "near"), axis=0, tiled=False)
    others = lax.ppermute(mine, "side", [(0, 1), (1, 0)])
    side = lax.axis_index("side").astype(jnp.int32).reshape(1)
    new_table = place(side, mine, others)
    return (new_table, new_moment_one, new_moment_two)


def solution(mesh):
    vocab, rep = mesh.devices.shape
    fours = Mesh(mesh.devices.reshape(vocab, rep // MEMBERS, MEMBERS // 2, 2), ALL)
    placed = (
        P(ALL),
        P(ALL, None),
        P("vocab", None),
        P(),
        P(ALL, None),
        P(ALL, None),
    )
    return jax.shard_map(
        on_device,
        mesh=fours,
        in_specs=placed,
        out_specs=(P("vocab", None), P(ALL, None), P(ALL, None)),
        check_vma=False,
    )
```

```python
import math

import jax
import jax.numpy as jnp
from jax import lax
from jax.experimental import pallas as pl
from jax.experimental.pallas import tpu as pltpu
from jax.sharding import Mesh
from jax.sharding import PartitionSpec as P

beta_one = 0.9
beta_two = 0.95
learn_rate = 0.01
decay_rate = 0.01
adam_eps = 1e-08
norm_eps = 1e-06
correct_one = 0.9999734386011124
correct_two = 0.9940794707920236

SLOTS = 4
LANES = 128
MEMBERS = 4
HIGH = 8
LOW = 16
CODE = 64


def pack_body(ids_hbm, cot_hbm, out_hbm, ids_ref, cot_ref, piece_ref, out_ref, sems, out_sems):
    tok_count, width = cot_ref.shape
    own = width // MEMBERS
    piece = own // 2
    _, owners, per_owner, lanes = out_ref.shape
    copy_ids = pltpu.make_async_copy(ids_hbm, ids_ref, sems.at[MEMBERS])
    copies = [
        pltpu.make_async_copy(
            cot_hbm.at[:, member * own : (member + 1) * own],
            cot_ref.at[:, member * own : (member + 1) * own],
            sems.at[member],
        )
        for member in range(MEMBERS)
    ]
    copy_ids.start()
    for copy in copies:
        copy.start()
    copy_ids.wait()
    ids_along = jnp.broadcast_to(ids_ref[...], (tok_count, tok_count))
    ids_down = ids_along.T
    down = lax.broadcasted_iota(jnp.int32, (tok_count, tok_count), 0)
    along = lax.broadcasted_iota(jnp.int32, (tok_count, tok_count), 1)
    earlier = ((ids_along >> 7) == (ids_down >> 7)) & (down < along)
    position = jnp.sum(earlier.astype(jnp.int32), axis=0, keepdims=True)
    slot = (ids_ref[...] >> 7) * per_owner + position
    slots = jnp.concatenate([slot, slot + SLOTS], axis=1)
    rows = lax.broadcasted_iota(jnp.int32, (owners * per_owner, 2 * tok_count), 0)
    picks = (rows == slots).astype(jnp.bfloat16)
    high = (ids_down >> 4) & (HIGH - 1)
    low = (ids_down & (LOW - 1)) + HIGH
    marks = [
        ((along == high + at) | (along == low + at)).astype(jnp.float32) for at in (CODE, 0)
    ]
    body = piece + CODE - LANES
    sends = []
    for member in range(MEMBERS):
        copies[member].wait()
        shared = cot_ref[:, (member + 1) * own - LANES : (member + 1) * own].astype(jnp.float32)
        for half in range(2):
            at = member * own + half * body
            rows_of = slice(half * tok_count, (half + 1) * tok_count)
            piece_ref[member, rows_of, :body] = cot_ref[:, at : at + body]
            piece_ref[member, rows_of, body:] = jnp.where(
                (along < CODE) == (half == 0), shared, marks[half]
            ).astype(jnp.bfloat16)
        moved = jnp.dot(picks, piece_ref[member], preferred_element_type=jnp.float32)
        out_ref[member] = moved.reshape(owners, per_owner, lanes).astype(jnp.bfloat16)
        sends.append(
            pltpu.make_async_copy(out_ref.at[member], out_hbm.at[:, member], out_sems.at[member])
        )
        sends[member].start()
    for send in sends:
        send.wait()


def pack(token_ids, cotangent, peer_count):
    tok_count, width = cotangent.shape
    lanes = width // (2 * MEMBERS) + CODE
    return pl.pallas_call(
        pack_body,
        in_specs=[pl.BlockSpec(memory_space=pl.ANY), pl.BlockSpec(memory_space=pl.ANY)],
        out_specs=pl.BlockSpec(memory_space=pl.ANY),
        out_shape=jax.ShapeDtypeStruct((peer_count, MEMBERS, 2 * SLOTS, lanes), jnp.bfloat16),
        scratch_shapes=[
            pltpu.VMEM((1, tok_count), jnp.int32),
            pltpu.VMEM((tok_count, width), jnp.bfloat16),
            pltpu.VMEM((MEMBERS, 2 * tok_count, lanes), jnp.bfloat16),
            pltpu.VMEM((MEMBERS, peer_count, 2 * SLOTS, lanes), jnp.bfloat16),
            pltpu.SemaphoreType.DMA((MEMBERS + 1,)),
            pltpu.SemaphoreType.DMA((MEMBERS,)),
        ],
        compiler_params=pltpu.CompilerParams(vmem_limit_bytes=58 * 1024 * 1024),
        cost_estimate=pl.CostEstimate(
            flops=2 * peer_count * 2 * SLOTS * 2 * tok_count * MEMBERS * lanes,
            bytes_accessed=2 * (tok_count * width + peer_count * MEMBERS * 2 * SLOTS * lanes),
            transcendentals=0,
        ),
        name="pack",
    )(token_ids.reshape(1, tok_count), cotangent)


def collect_body(part_ref, out_ref):
    body = part_ref.shape[1] - LANES
    shard_row = lax.broadcasted_iota(jnp.int32, (LANES, LANES), 0)
    lane = lax.broadcasted_iota(jnp.int32, (LANES, LANES), 1)
    high = shard_row >> 4
    low = (shard_row & (LOW - 1)) + HIGH
    digits = jnp.concatenate(
        [(lane == value).astype(jnp.bfloat16) for value in (high + CODE, high, low + CODE, low)],
        axis=0,
    )
    found = lax.dot_general(
        digits,
        part_ref[:, body:],
        (((1,), (1,)), ((), ())),
        preferred_element_type=jnp.float32,
    )
    half = lax.broadcasted_iota(jnp.int32, (LANES, found.shape[1]), 1) & SLOTS
    first = jnp.where(half == 0, found[:LANES] * found[2 * LANES : 3 * LANES], 0.0)
    second = jnp.where(half == 0, 0.0, found[LANES : 2 * LANES] * found[3 * LANES :])
    picks = jnp.concatenate([first, second], axis=0).astype(jnp.bfloat16)
    sums = jnp.dot(picks, part_ref[...], preferred_element_type=jnp.float32)
    out_ref[:, :body] = sums[:LANES, :body].astype(jnp.bfloat16)
    out_ref[:, body : 2 * body] = sums[LANES:, :body].astype(jnp.bfloat16)
    out_ref[:, 2 * body :] = jnp.where(lane < CODE, sums[:LANES, body:], sums[LANES:, body:]).astype(
        jnp.bfloat16
    )


def collect(arrived):
    count, lanes = arrived.shape
    piece = lanes - CODE
    return pl.pallas_call(
        collect_body,
        in_specs=[pl.BlockSpec(memory_space=pltpu.VMEM)],
        out_specs=pl.BlockSpec(memory_space=pltpu.VMEM),
        out_shape=jax.ShapeDtypeStruct((LANES, 2 * piece), jnp.bfloat16),
        compiler_params=pltpu.CompilerParams(vmem_limit_bytes=40 * 1024 * 1024),
        cost_estimate=pl.CostEstimate(
            flops=2 * count * 2 * LANES * lanes,
            bytes_accessed=2 * (count * lanes + 2 * LANES * piece),
            transcendentals=0,
        ),
        name="collect",
    )(arrived)


def adam_body(rep_ref, sum_ref, table_ref, gain_ref, one_ref, two_ref, up_ref, one_out, two_out):
    width = table_ref.shape[1]
    root = math.sqrt(width)
    params = table_ref[...].astype(jnp.float32)
    scaled = params * root
    rows = table_ref.shape[0]
    totals = []
    for member in range(MEMBERS):
        total = sum_ref[member * rows : (member + 1) * rows, :].astype(jnp.float32)
        for peer in range(member + MEMBERS, sum_ref.shape[0] // rows, MEMBERS):
            total = total + sum_ref[peer * rows : (peer + 1) * rows, :].astype(jnp.float32)
        totals.append(total)
    weighted = jnp.concatenate(totals, axis=1) * gain_ref[...]
    mean_square = jnp.mean(scaled * scaled, axis=-1, keepdims=True)
    inverse = lax.rsqrt(mean_square + norm_eps)
    inner_mean = jnp.mean(scaled * weighted, axis=-1, keepdims=True)
    grad = root * inverse * (weighted - scaled * (inverse * inverse * inner_mean))
    new_one = beta_one * one_ref[...] + (1.0 - beta_one) * grad
    new_two = beta_two * two_ref[...] + (1.0 - beta_two) * grad * grad
    one_out[...] = new_one
    two_out[...] = new_two
    update = (
        new_one / correct_one / (jnp.sqrt(new_two / correct_two) + adam_eps) + decay_rate * params
    )
    up_ref[...] = (params - learn_rate * update).astype(jnp.bfloat16)


def adam(rep_index, partial_sums, embed_table, norm_gain, moment_one, moment_two):
    rows, width = moment_one.shape
    peers = embed_table.shape[0] // rows
    whole = pl.BlockSpec((rows, width), lambda i, rep: (0, 0))
    return pl.pallas_call(
        adam_body,
        grid_spec=pltpu.PrefetchScalarGridSpec(
            num_scalar_prefetch=1,
            grid=(1,),
            in_specs=[
                pl.BlockSpec((peers * rows, width // MEMBERS), lambda i, rep: (0, 0)),
                pl.BlockSpec((rows, width), lambda i, rep: (rep[0], 0)),
                pl.BlockSpec((1, width), lambda i, rep: (0, 0)),
                whole,
                whole,
            ],
            out_specs=[whole, whole, whole],
        ),
        out_shape=[
            jax.ShapeDtypeStruct((rows, width), jnp.bfloat16),
            jax.ShapeDtypeStruct((rows, width), jnp.float32),
            jax.ShapeDtypeStruct((rows, width), jnp.float32),
        ],
        compiler_params=pltpu.CompilerParams(vmem_limit_bytes=40 * 1024 * 1024),
        cost_estimate=pl.CostEstimate(
            flops=40 * rows * width, bytes_accessed=24 * rows * width, transcendentals=rows * width
        ),
        name="adam",
    )(rep_index, partial_sums, embed_table, norm_gain.reshape(1, width), moment_one, moment_two)


def place_body(side_ref, mine_ref, others_ref, out_hbm, sems):
    count, rows, _ = mine_ref.shape
    side = side_ref[0]
    copies = []
    for at in range(count):
        for which, source in enumerate((mine_ref, others_ref)):
            parity = side if which == 0 else 1 - side
            start = pl.multiple_of((2 * at + parity) * rows, rows)
            copies.append(
                pltpu.make_async_copy(
                    source.at[at], out_hbm.at[pl.ds(start, rows), :], sems.at[2 * at + which]
                )
            )
    for copy in copies:
        copy.start()
    for copy in copies:
        copy.wait()


def place(side, mine, others):
    count, rows, width = mine.shape
    return pl.pallas_call(
        place_body,
        in_specs=[
            pl.BlockSpec(memory_space=pltpu.SMEM),
            pl.BlockSpec(memory_space=pltpu.VMEM),
            pl.BlockSpec(memory_space=pltpu.VMEM),
        ],
        out_specs=pl.BlockSpec(memory_space=pl.ANY),
        out_shape=jax.ShapeDtypeStruct((2 * count * rows, width), mine.dtype),
        scratch_shapes=[pltpu.SemaphoreType.DMA((2 * count,))],
        compiler_params=pltpu.CompilerParams(vmem_limit_bytes=24 * 1024 * 1024),
        cost_estimate=pl.CostEstimate(
            flops=0, bytes_accessed=8 * count * rows * width, transcendentals=0
        ),
        name="place",
    )(side, mine, others)


REP = ("far", "near", "side")
ALL = ("vocab", "far", "near", "side")


def on_device(token_ids, cotangent, embed_table, norm_gain, moment_one, moment_two):
    peer_count = lax.axis_size("vocab")
    outgoing = pack(token_ids, cotangent, peer_count)
    outgoing = outgoing.reshape(-1, outgoing.shape[-1])
    arrived = lax.all_to_all(outgoing, ("vocab", "near", "side"), split_axis=0, concat_axis=0, tiled=True)
    row_sum = collect(arrived)
    partial_sums = lax.all_to_all(row_sum, REP, split_axis=0, concat_axis=0, tiled=True)
    rep_index = lax.axis_index(REP).astype(jnp.int32).reshape(1)
    updated, new_moment_one, new_moment_two = adam(
        rep_index, partial_sums, embed_table, norm_gain, moment_one, moment_two
    )
    mine = lax.all_gather(updated, ("far", "near"), axis=0, tiled=False)
    others = lax.ppermute(mine, "side", [(0, 1), (1, 0)])
    side = lax.axis_index("side").astype(jnp.int32).reshape(1)
    new_table = place(side, mine, others)
    return (new_table, new_moment_one, new_moment_two)


def solution(mesh):
    vocab, rep = mesh.devices.shape
    fours = Mesh(mesh.devices.reshape(vocab, rep // MEMBERS, MEMBERS // 2, 2), ALL)
    placed = (
        P(ALL),
        P(ALL, None),
        P("vocab", None),
        P(),
        P(ALL, None),
        P(ALL, None),
    )
    return jax.shard_map(
        on_device,
        mesh=fours,
        in_specs=placed,
        out_specs=(P("vocab", None), P(ALL, None), P(ALL, None)),
        check_vma=False,
    )
```
